512 devices in a mesh: seq: 64 (over z_hi, x, y), head: 8 (over z_lo, core).
Axes of the slice: x: 4, y: 8, z: 8 (z_hi: 2, z_lo: 4; z = z_hi * 4 + z_lo), core: 2. Of those that a mesh axis runs over, the one named last changes fastest.
Arguments:
- queries: bfloat16 [24576, 8192], P(('seq', 'head')), may hold values from -16 to 16
- keys: bfloat16 [24576, 1024], P(('seq', 'head')), may hold values from -16 to 16
- values: bfloat16 [24576, 1024], P(('seq', 'head')), may hold values from -6 to 6
- output_cotangent: bfloat16 [24576, 8192], P(('seq', 'head')), may hold values from -6 to 6
- doc_ids: int32 [24576], replicated, may hold values from 0 to 255, never falling along the last dimension, each value on 1 to 768 neighbouring positions
Outputs:
- attention_out: bfloat16 [24576, 8192], P(('seq', 'head'))
- query_grad: bfloat16 [24576, 8192], P(('seq', 'head'))
- key_gradient: bfloat16 [24576, 1024], P(('seq', 'head'))
- value_gradient: bfloat16 [24576, 1024], P(('seq', 'head'))
The draws below stay inside these ranges and needn't reach their ends.
Inputs may be any that keep to these rules, and one draw needn't show every extreme that they name: `doc_ids`: document numbers never fall along the sequence; a document holds at most 768 tokens, and one holds exactly 768.
All inputs are finite; a program needn't handle non-finite values.
Results may differ from the reference program's by a relative error of at most 0.03.
Values may be sent and summed in bfloat16 or wider, within the bound.
A program may use at most 128 MiB of HBM per device.

```python
import math
import jax
import jax.numpy as jnp
import numpy as np
from jax import lax

QUERY_HEADS = 64
KEY_VALUE_HEADS = 8
HEAD_SIZE = 128
TOKENS_PER_SHARD = 384
DOCUMENT_LIMIT = 768
PACKED_TOKENS = 24576
DOCS = 256


def draw_queries(key, part):
    key = jax.random.fold_in(key, 11)
    starting_rows = jnp.clip(jax.random.normal(key, (PACKED_TOKENS, QUERY_HEADS * HEAD_SIZE), jnp.float32), -6.0, 6.0)
    return starting_rows.astype(jnp.bfloat16)


def draw_keys(key, part):
    key = jax.random.fold_in(key, 12)
    starting_rows = jnp.clip(jax.random.normal(key, (PACKED_TOKENS, KEY_VALUE_HEADS * HEAD_SIZE), jnp.float32), -6.0, 6.0)
    return starting_rows.astype(jnp.bfloat16)


def level_of(key, extent, cuts, smallest, top_value):
    gain = 1.0
    for dim, blocks in cuts:
        heights = jax.random.uniform(jax.random.fold_in(jax.random.fold_in(key, 6), dim), (blocks,), jnp.float32, smallest / len(cuts), top_value / len(cuts))
        gain = gain * jnp.repeat(jnp.exp(heights), extent[dim] // blocks).reshape((-1,) + (1,) * (len(extent) - 1 - dim))
    return gain


def length_profile(amount, total, limit, lean):
    weights = [(1 << 20) // math.isqrt(rank ** lean) + 1 for rank in range(2, amount + 1)]
    spare, counts = total - limit - (amount - 1), [1] * (amount - 1)
    while spare > 0:
        candidates = [i for i in range(amount - 1) if counts[i] < limit]
        pool, remaining = sum([weights[i] for i in candidates]), spare
        for i in candidates:
            addition = min(limit - counts[i], max(1, remaining * weights[i] // pool), spare)
            counts[i] = counts[i] + addition
            spare = spare - addition
    return np.array([limit] + counts)


def uneven(stream_key, amount, total, bound, lean):
    if amount == 2:
        one = jax.random.randint(stream_key, (), max(1, total - bound), min(bound, total - 1) + 1)
        return jnp.stack([one, total - one])
    sizes = jnp.asarray(length_profile(amount, total, bound, lean), jnp.int32)
    couples = (amount - 1) // 2
    giver, sink = sizes[1:1 + 2 * couples:2], sizes[2:2 + 2 * couples:2]
    margin = jnp.minimum(giver - 1, bound - sink)
    shifted = jax.random.randint(jax.random.fold_in(stream_key, 1), (couples,), 0, 1 << 20) % (margin + 1)
    sizes = sizes.at[1:1 + 2 * couples:2].set(giver - shifted).at[2:2 + 2 * couples:2].set(sink + shifted)
    return sizes[jax.random.permutation(jax.random.fold_in(stream_key, 2), amount)]


def normal_values(stream_key, dims, deviation, limit, cuts=(), held_as=jnp.bfloat16):
    drawn = jax.random.normal(stream_key, dims, jnp.float32) * deviation
    if len(cuts) > 0:
        drawn = level_of(stream_key, dims, cuts, -0.22, 0.18) * drawn
    return jnp.clip(drawn, min=-limit, max=limit).astype(held_as)


def setup_inputs(seed: int = 0) -> dict:
    arg_keys = jax.random.split(jax.random.key(seed), 6)
    queries = draw_queries(jax.random.fold_in(arg_keys[5], 71), 0)
    keys = draw_keys(jax.random.fold_in(arg_keys[5], 71), 0)
    values = normal_values(arg_keys[2], (PACKED_TOKENS, KEY_VALUE_HEADS * HEAD_SIZE), 1.0, 6.0, ((0, 512),))
    output_cotangent = normal_values(arg_keys[3], (PACKED_TOKENS, QUERY_HEADS * HEAD_SIZE), 1.0, 6.0, ((0, 512),))
    doc_ids = jnp.searchsorted(jnp.cumsum(uneven(arg_keys[4], DOCS, PACKED_TOKENS, DOCUMENT_LIMIT, 2)), jnp.arange(PACKED_TOKENS), side="right").astype(jnp.int32)
    return dict(queries=queries, keys=keys, values=values, output_cotangent=output_cotangent, doc_ids=doc_ids)


def reference(queries, keys, values, output_cotangent, doc_ids):
    group_repeat = QUERY_HEADS // KEY_VALUE_HEADS
    scale = HEAD_SIZE ** -0.5
    win_rows = TOKENS_PER_SHARD + DOCUMENT_LIMIT
    block_total = PACKED_TOKENS // TOKENS_PER_SHARD
    leading_rows = jnp.zeros((DOCUMENT_LIMIT, KEY_VALUE_HEADS, HEAD_SIZE), keys.dtype)
    key_padding = jnp.concatenate([leading_rows, keys.reshape(PACKED_TOKENS, KEY_VALUE_HEADS, HEAD_SIZE)], 0)
    value_padding = jnp.concatenate([leading_rows, values.reshape(PACKED_TOKENS, KEY_VALUE_HEADS, HEAD_SIZE)], 0)
    id_pad = jnp.concatenate([jnp.full((DOCUMENT_LIMIT,), -1, jnp.int32), doc_ids.astype(jnp.int32)], 0)
    query_tiles_list = queries.reshape(block_total, TOKENS_PER_SHARD, KEY_VALUE_HEADS, group_repeat, HEAD_SIZE)
    cotangent_blocks = output_cotangent.reshape(block_total, TOKENS_PER_SHARD, KEY_VALUE_HEADS, group_repeat, HEAD_SIZE)
    id_blocks = doc_ids.astype(jnp.int32).reshape(block_total, TOKENS_PER_SHARD)
    query_place = DOCUMENT_LIMIT + jnp.arange(TOKENS_PER_SHARD, dtype=jnp.int32)
    key_place = jnp.arange(win_rows, dtype=jnp.int32)
    causal = key_place[None, :] <= query_place[:, None]

    def block_step(carry_pair, inputs):
        key_running_sum, value_running_sum = carry_pair
        block_index, query_block, cot_block, query_ids = inputs
        offset = (block_index * TOKENS_PER_SHARD).astype(jnp.int32)
        key_win = lax.dynamic_slice_in_dim(key_padding, offset, win_rows, 0).astype(jnp.float32)
        value_win = lax.dynamic_slice_in_dim(value_padding, offset, win_rows, 0).astype(jnp.float32)
        key_ids = lax.dynamic_slice_in_dim(id_pad, offset, win_rows, 0)
        allowed = causal & (query_ids[:, None] == key_ids[None, :])
        query_full = query_block.astype(jnp.float32)
        cot_full = cot_block.astype(jnp.float32)
        scores = jnp.einsum("qgrd,kgd->grqk", query_full, key_win) * scale
        scores = jnp.where(allowed, scores, -jnp.inf)
        top_score = jnp.max(scores, -1, keepdims=True)
        log_total = top_score + jnp.log(jnp.sum(jnp.exp(scores - top_score), -1, keepdims=True))
        probs = jnp.exp(scores - log_total)
        probs_half = lax.optimization_barrier(probs.astype(jnp.bfloat16)).astype(jnp.float32)
        attended = jnp.einsum("grqk,kgd->qgrd", probs_half, value_win).astype(jnp.bfloat16)
        delta_rows = jnp.einsum("qgrd,qgrd->grq", attended.astype(jnp.float32), cot_full)
        prob_grad = jnp.einsum("qgrd,kgd->grqk", cot_full, value_win)
        score_grad = probs * (prob_grad - delta_rows[..., None]) * scale
        score_grad = lax.optimization_barrier(score_grad.astype(jnp.bfloat16)).astype(jnp.float32)
        grad_query = jnp.einsum("grqk,kgd->qgrd", score_grad, key_win).astype(jnp.bfloat16)
        key_part = jnp.einsum("grqk,qgrd->kgd", score_grad, query_full)
        value_part = jnp.einsum("grqk,qgrd->kgd", probs_half, cot_full)
        key_running_sum = lax.dynamic_update_slice_in_dim(key_running_sum, lax.dynamic_slice_in_dim(key_running_sum, offset, win_rows, 0) + key_part, offset, 0)
        value_running_sum = lax.dynamic_update_slice_in_dim(value_running_sum, lax.dynamic_slice_in_dim(value_running_sum, offset, win_rows, 0) + value_part, offset, 0)
        return (key_running_sum, value_running_sum), (attended, grad_query)

    empty_running_sum = jnp.zeros((PACKED_TOKENS + DOCUMENT_LIMIT, KEY_VALUE_HEADS, HEAD_SIZE), jnp.float32)
    steps_in = (jnp.arange(block_total, dtype=jnp.int32), query_tiles_list, cotangent_blocks, id_blocks)
    (key_running_sum, value_running_sum), (attended, grad_query) = lax.scan(block_step, (empty_running_sum, empty_running_sum), steps_in)
    attention_out = attended.reshape(PACKED_TOKENS, QUERY_HEADS * HEAD_SIZE)
    query_grad = grad_query.reshape(PACKED_TOKENS, QUERY_HEADS * HEAD_SIZE)
    key_gradient = key_running_sum[DOCUMENT_LIMIT:].reshape(PACKED_TOKENS, KEY_VALUE_HEADS * HEAD_SIZE).astype(jnp.bfloat16)
    value_gradient = value_running_sum[DOCUMENT_LIMIT:].reshape(PACKED_TOKENS, KEY_VALUE_HEADS * HEAD_SIZE).astype(jnp.bfloat16)
    return (attention_out, query_grad, key_gradient, value_gradient)
```

```python
import functools
import math

import jax
import jax.numpy as jnp
from jax import lax
from jax.experimental import pallas as pl
from jax.experimental.pallas import tpu as pltpu
from jax.sharding import PartitionSpec as P

MESH = pl.DeviceIdType.MESH
HEAD_SIZE = 128
SLOTS = 8
LINE = 4
SCALE = HEAD_SIZE**-0.5
TILE = 256
HIDDEN = -1e30


def dot(left, right, left_dim, right_dim):
    return lax.dot_general(
        left, right, (((left_dim,), (right_dim,)), ((), ())), preferred_element_type=jnp.float32
    )


def kernel(
    shards, groups, repeat, rows,
    q_ref, k_ref, v_ref, c_ref, bounds_ref,
    out_ref, dq_ref, dk_ref, dv_ref,
    qb, cb, ob, gb, kv, bias, acc, qs, cs, os, gs, stage, from_next, from_up, from_down,
    x_send, x_recv, x_local, o_send, o_recv, o_local,
    send_next, send_up, send_down, slot_recv, grad_send, next_recv, up_recv, down_recv,
):
    block = 2 * rows
    window = (SLOTS + 1) * block
    stacked = repeat * block
    wide = repeat * HEAD_SIZE
    s, h = lax.axis_index("seq"), lax.axis_index("head")
    z, k = lax.div(h, 2), lax.rem(h, 2)
    sibling = (s, h + 1 - 2 * k)
    half = shards // 2
    first, cross = s == 0, s == half
    gate = (s == half - 1) & (z == LINE - 1)
    entry = cross & (z == 0)
    has_next = (s < shards - 1) & (s != half - 1)
    has_prev = (s > 0) & (s != half)
    gate_int = gate.astype(jnp.int32)
    entry_int = entry.astype(jnp.int32)
    up = (s + gate_int, h + 2 - gate_int * 2 * LINE)
    down = (s - entry_int, h - 2 + entry_int * 2 * LINE)
    later, earlier = (s + 1, h), (s - 1, h)

    def exists(j):
        return s * LINE + z >= j

    def goes_next(j):
        return has_next & exists(j) if j <= LINE else None

    def goes_up(j):
        if j > SLOTS - 1:
            return None
        chain = gate | (cross & (z < LINE - 1))
        return chain | ((z < LINE - 1) & (z >= j)) if j < LINE else chain

    def goes_down(j):
        if j < 2 or j > LINE:
            return None
        return (z > 0) & (z < j) & jnp.logical_not(cross | first)

    def comes_up(j):
        return (z >= j) | cross

    def comes_down(j):
        return (z < j) & jnp.logical_not(cross | first)

    def slot(g, j):
        return kv.at[g, :, pl.ds((SLOTS - j) * block, block), :]

    def remote(src, dst, send, recv, device):
        return pltpu.make_async_remote_copy(
            src_ref=src, dst_ref=dst, send_sem=send, recv_sem=recv,
            device_id=device, device_id_type=MESH,
        )

    def when(condition, work):
        if condition is not None:
            pl.when(condition)(work)

    def columns(core, g, width):
        start = (core * groups + g) * width
        return pl.ds(pl.multiple_of(start, HEAD_SIZE), width)

    mine = pl.ds(pl.multiple_of(k * rows, 16), rows)
    theirs = pl.ds(pl.multiple_of((1 - k) * rows, 16), rows)
    mine_tail = pl.ds(pl.multiple_of(SLOTS * block + k * rows, 16), rows)

    def in_place(index, g):
        return (
            lambda: qb.at[g, mine, :], lambda: cb.at[g, mine, :],
            lambda: kv.at[g, 0, mine_tail, :], lambda: kv.at[g, 1, mine_tail, :],
        )[index]()

    def in_copies(index, g):
        source = (q_ref, c_ref, k_ref, v_ref)[index]
        width = wide if index < 2 else HEAD_SIZE
        local = pltpu.make_async_copy(
            source.at[:, columns(k, g, width)], in_place(index, g), x_local.at[g, index]
        )
        over = remote(
            source.at[:, columns(1 - k, g, width)], in_place(index, g),
            x_send.at[g, index], x_recv.at[g, index], sibling,
        )
        return local, over

    def start_in(index, g):
        local, over = in_copies(index, g)
        over.start()
        local.start()

    def wait_in(index, g):
        local, over = in_copies(index, g)
        local.wait()
        over.wait()

    def out_copies(index, g):
        target = (out_ref, dq_ref, dk_ref, dv_ref)[index]
        width = wide if index < 2 else HEAD_SIZE

        def part(which):
            if index < 2:
                return (ob, gb)[index].at[g, which, :]
            return stage.at[g, 0, index - 2, which, :]

        place = target.at[:, columns(k, g, width)]
        local = pltpu.make_async_copy(part(mine), place, o_local.at[g, index])
        over = remote(part(theirs), place, o_send.at[g, index], o_recv.at[g, index], sibling)
        return local, over

    def start_out(index, g):
        local, over = out_copies(index, g)
        over.start()
        local.start()

    def wait_out(index, g):
        local, over = out_copies(index, g)
        local.wait()
        over.wait()

    def next_copy(g, j):
        return remote(
            slot(g, j), slot(g, j + LINE), send_next.at[g, j], slot_recv.at[g, j + LINE], later
        )

    def up_copy(g, j):
        return remote(slot(g, j), slot(g, j + 1), send_up.at[g, j], slot_recv.at[g, j + 1], up)

    def down_copy(g, j):
        return remote(
            slot(g, j), slot(g, j - 1), send_down.at[g, j], slot_recv.at[g, j - 1], down
        )

    def forward(g, j):
        when(goes_next(j), lambda: next_copy(g, j).start())
        when(goes_up(j), lambda: up_copy(g, j).start())
        when(goes_down(j), lambda: down_copy(g, j).start())

    def relay(g, j, condition):
        def work():
            remote(
                slot(g, j), slot(g, j), send_next.at[g, 0], slot_recv.at[g, j], sibling
            ).wait_recv()
            forward(g, j)

        when(condition, work)

    def relay_part(g, part):
        if part == 0:
            relay(g, 1, comes_up(1))
            relay(g, 4, exists(4))
        elif part == 1:
            relay(g, 2, comes_up(2))
            relay(g, 3, comes_down(3))
            relay(g, 3, comes_up(3))
        else:
            relay(g, 2, comes_down(2))
            relay(g, 1, comes_down(1))
            for j in range(LINE + 1, SLOTS + 1):
                relay(g, j, exists(j))

    def own(g):
        wait_in(2, g)
        wait_in(3, g)
        forward(g, 0)

    def span(j):
        return pl.ds((SLOTS - j) * block, block)

    def add(g, j, source, index, sem):
        remote(source.at[g, index], source.at[g, index], grad_send.at[g, 0], sem, sibling).wait_recv()
        acc[g, :, span(j), :] += source[g, index].astype(jnp.float32)

    def give(g, j, place, sem, device):
        return remote(stage.at[g, j], place, grad_send.at[g, j], sem, device)

    def to_down(g, j):
        return give(g, j, from_up.at[g, j - 1], up_recv.at[g, j - 1], down)

    def to_up(g, j):
        return give(g, j, from_down.at[g, j - 1], down_recv.at[g, j - 1], up)

    def to_earlier(g, j):
        return give(g, j, from_next.at[g, j - LINE], next_recv.at[g, j - LINE], earlier)

    def send_back(g, j, action):
        if j < LINE:
            pl.when(comes_up(j))(lambda: action(to_down(g, j)))
            pl.when(comes_down(j))(lambda: action(to_up(g, j)))
        else:
            pl.when(cross)(lambda: action(to_down(g, j)))
            pl.when(has_prev & exists(j))(lambda: action(to_earlier(g, j)))

    def give_back(g, j, condition):
        def work():
            when(goes_next(j), lambda: add(g, j, from_next, j, next_recv.at[g, j]))
            when(goes_up(j), lambda: add(g, j, from_up, j, up_recv.at[g, j]))
            when(goes_down(j), lambda: add(g, j, from_down, j - 2, down_recv.at[g, j - 2]))
            total = acc[g, :, span(j), :]
            if j == 0:
                stage[g, 0, 0] = (total[0] * SCALE).astype(jnp.bfloat16)
                stage[g, 0, 1] = total[1].astype(jnp.bfloat16)
                start_out(2, g)
                start_out(3, g)
            else:
                stage[g, j] = total.astype(jnp.bfloat16)
                send_back(g, j, lambda copy: copy.start())

        when(condition, work)

    def leaves(g):
        for j in range(SLOTS, LINE, -1):
            chained = goes_up(j)
            free = exists(j) if chained is None else exists(j) & jnp.logical_not(chained)
            give_back(g, j, free)

    def inner(g):
        for j in range(SLOTS - 1, LINE, -1):
            give_back(g, j, goes_up(j))
        for j in range(1, LINE):
            give_back(g, j, comes_down(j))
        give_back(g, LINE, exists(LINE))
        for j in range(LINE - 1, 0, -1):
            give_back(g, j, comes_up(j))
        give_back(g, 0, s >= 0)

    def gather_rows(g):
        wait_in(0, g)
        wait_in(1, g)
        for r in range(repeat):
            place = pl.ds(r * block, block)
            cols = pl.ds(r * HEAD_SIZE, HEAD_SIZE)
            qs[place, :] = qb[g, :, cols]
            cs[place, :] = cb[g, :, cols]

    def spread_rows(g):
        for r in range(repeat):
            place = pl.ds(r * block, block)
            cols = pl.ds(r * HEAD_SIZE, HEAD_SIZE)
            ob[g, :, cols] = os[place, :]
            gb[g, :, cols] = gs[place, :]
        start_out(0, g)
        start_out(1, g)

    def tile(g, n):
        place = pl.ds(n * TILE, TILE)
        query, cot = qs[place, :], cs[place, :]
        key, value = kv[g, 0], kv[g, 1]
        scores = dot(key, query, 1, 1) * (SCALE * math.log2(math.e)) + bias[:, place]
        top = jnp.max(scores, 0, keepdims=True)
        e = jnp.exp2(scores - top)
        inverse = 1.0 / jnp.sum(e, 0, keepdims=True)
        e_half = e.astype(jnp.bfloat16)
        cot_t = (cot.astype(jnp.float32).T * inverse).astype(jnp.bfloat16)
        out_t = dot(value, e_half, 0, 0) * inverse
        out_half = out_t.astype(jnp.bfloat16).astype(jnp.float32)
        delta = jnp.sum(out_half * cot_t.astype(jnp.float32), 0, keepdims=True)
        score_grad = (e * (dot(value, cot_t, 1, 0) - delta)).astype(jnp.bfloat16)
        query_grad_t = dot(key, score_grad, 0, 0) * SCALE
        acc[g, 0] += dot(score_grad, query, 1, 0)
        acc[g, 1] += dot(e_half, cot_t, 1, 1)
        os[place, :] = out_half.T.astype(jnp.bfloat16)
        gs[place, :] = query_grad_t.T.astype(jnp.bfloat16)

    barrier = pltpu.get_barrier_semaphore()

    def greet(device):
        pl.semaphore_signal(barrier, inc=1, device_id=device, device_id_type=MESH)

    has_up = (z < LINE - 1) | gate
    has_down = (z > 0) | entry
    greet(sibling)
    pl.when(has_up)(lambda: greet(up))
    pl.when(has_down)(lambda: greet(down))
    pl.when(has_next)(lambda: greet(later))
    pl.when(has_prev)(lambda: greet(earlier))
    friends = 1
    for there in (has_up, has_down, has_next, has_prev):
        friends = friends + there.astype(jnp.int32)
    pl.semaphore_wait(barrier, friends)

    def open_group(g, _):
        start_in(2, g)
        start_in(3, g)
        return _

    def open_rows(g, _):
        start_in(0, g)
        start_in(1, g)
        for j in range(1, SLOTS + 1):

            def blank(j=j):
                kv[g, :, span(j), :] = jnp.zeros((2, block, HEAD_SIZE), jnp.bfloat16)

            pl.when(jnp.logical_not(exists(j)))(blank)
        return _

    lax.fori_loop(0, groups, open_group, 0)
    lax.fori_loop(0, groups, open_rows, 0)
    own(0)

    def clear(g, _):
        acc[g] = jnp.zeros((2, window, HEAD_SIZE), jnp.float32)
        return _

    lax.fori_loop(0, groups, clear, 0)
    place = lax.broadcasted_iota(jnp.int32, (window, stacked), 0)
    seen = (place >= bounds_ref[0:1, :]) & (place <= bounds_ref[1:2, :])
    bias[...] = jnp.where(seen, 0.0, HIDDEN)

    tiles = stacked // TILE

    def step(i, _):
        working = (i >= 1) & (i <= groups)

        @pl.when(i + 1 < groups)
        def _():
            own(i + 1)

        @pl.when(working)
        def _():
            gather_rows(i - 1)

        def inside(n, _):
            @pl.when(working)
            def _():
                tile(i - 1, n)

            for part in range(3):

                @pl.when((i < groups) & (n == part))
                def _(part=part):
                    relay_part(i, part)

            return 0

        lax.fori_loop(0, tiles, inside, 0)

        @pl.when(working)
        def _():
            spread_rows(i - 1)
            leaves(i - 1)

        @pl.when(i >= 2)
        def _():
            inner(i - 2)

        return 0

    lax.fori_loop(0, groups + 2, step, 0)

    def close(g, _):
        for index in range(4):
            wait_out(index, g)
        for j in range(SLOTS + 1):
            when(goes_next(j), lambda: next_copy(g, j).wait_send())
            when(goes_up(j), lambda: up_copy(g, j).wait_send())
            when(goes_down(j), lambda: down_copy(g, j).wait_send())
            if j > 0:
                send_back(g, j, lambda copy: copy.wait_send())
        return 0

    lax.fori_loop(0, groups, close, 0)


def shard(queries, keys, values, output_cotangent, doc_ids):
    shards = lax.axis_size("seq")
    rows = queries.shape[0]
    block = 2 * rows
    window = (SLOTS + 1) * block
    groups = keys.shape[1] // HEAD_SIZE // 2
    repeat = queries.shape[1] // keys.shape[1]
    stacked = repeat * block
    wide = repeat * HEAD_SIZE

    origin = (lax.axis_index("seq") * LINE + lax.axis_index("head") // 2) * block
    base = jnp.maximum(origin - SLOTS * block, 0)
    near = lax.dynamic_slice(doc_ids, (base,), (window,))
    here = lax.dynamic_slice(doc_ids, (origin,), (block,))
    begin = base + jnp.sum((near[None, :] < here[:, None]).astype(jnp.int32), 1)
    begin = begin - (origin - SLOTS * block)
    end = SLOTS * block + jnp.arange(block, dtype=jnp.int32)
    bounds = jnp.stack([jnp.tile(begin, repeat), jnp.tile(end, repeat)])

    bf16, f32 = jnp.bfloat16, jnp.float32
    any_spec = pl.BlockSpec(memory_space=pl.ANY)
    dma = pltpu.SemaphoreType.DMA
    pair = (2, block, HEAD_SIZE)
    return pl.pallas_call(
        functools.partial(kernel, shards, groups, repeat, rows),
        out_shape=(
            jax.ShapeDtypeStruct(queries.shape, bf16),
            jax.ShapeDtypeStruct(queries.shape, bf16),
            jax.ShapeDtypeStruct(keys.shape, bf16),
            jax.ShapeDtypeStruct(keys.shape, bf16),
        ),
        in_specs=[any_spec] * 4 + [pl.BlockSpec(memory_space=pltpu.VMEM)],
        out_specs=[any_spec] * 4,
        scratch_shapes=[
            pltpu.VMEM((groups, block, wide), bf16),
            pltpu.VMEM((groups, block, wide), bf16),
            pltpu.VMEM((groups, block, wide), bf16),
            pltpu.VMEM((groups, block, wide), bf16),
            pltpu.VMEM((groups, 2, window, HEAD_SIZE), bf16),
            pltpu.VMEM((window, stacked), f32),
            pltpu.VMEM((groups, 2, window, HEAD_SIZE), f32),
            pltpu.VMEM((stacked, HEAD_SIZE), bf16),
            pltpu.VMEM((stacked, HEAD_SIZE), bf16),
            pltpu.VMEM((stacked, HEAD_SIZE), bf16),
            pltpu.VMEM((stacked, HEAD_SIZE), bf16),
            pltpu.VMEM((groups, SLOTS + 1) + pair, bf16),
            pltpu.VMEM((groups, LINE + 1) + pair, bf16),
            pltpu.VMEM((groups, SLOTS) + pair, bf16),
            pltpu.VMEM((groups, LINE - 1) + pair, bf16),
            dma((groups, 4)), dma((groups, 4)), dma((groups, 4)),
            dma((groups, 4)), dma((groups, 4)), dma((groups, 4)),
            dma((groups, LINE + 1)), dma((groups, SLOTS)), dma((groups, LINE + 1)),
            dma((groups, SLOTS + 1)), dma((groups, SLOTS + 1)),
            dma((groups, LINE + 1)), dma((groups, SLOTS)), dma((groups, LINE - 1)),
        ],
        compiler_params=pltpu.CompilerParams(
            collective_id=0, has_side_effects=True, vmem_limit_bytes=56 * 1024 * 1024
        ),
    )(queries, keys, values, output_cotangent, bounds)


def solution(mesh):
    tokens = P(("seq", "head"), None)
    return jax.shard_map(
        shard,
        mesh=mesh,
        in_specs=(tokens, tokens, tokens, tokens, P()),
        out_specs=(tokens, tokens, tokens, tokens),
        check_vma=False,
    )
```

```python
import functools
import math

import jax
import jax.numpy as jnp
from jax import lax
from jax.experimental import pallas as pl
from jax.experimental.pallas import tpu as pltpu
from jax.sharding import PartitionSpec as P

MESH = pl.DeviceIdType.MESH
HEAD_SIZE = 128
SLOTS = 8
LINE = 4
SCALE = HEAD_SIZE**-0.5
TILE = 256
HIDDEN = -1e30


def dot(left, right, left_dim, right_dim):
    return lax.dot_general(
        left, right, (((left_dim,), (right_dim,)), ((), ())), preferred_element_type=jnp.float32
    )


def kernel(
    shards, groups, repeat, rows,
    q_ref, k_ref, v_ref, c_ref, bounds_ref,
    out_ref, dq_ref, dk_ref, dv_ref,
    qb, cb, ob, gb, kv, bias, acc, qs, cs, os, gs, stage, from_next, from_up, from_down,
    x_send, x_recv, x_local, o_send, o_recv, o_local,
    send_next, send_up, send_down, slot_recv, grad_send, next_recv, up_recv, down_recv,
):
    block = 2 * rows
    window = (SLOTS + 1) * block
    stacked = repeat * block
    wide = repeat * HEAD_SIZE
    s, h = lax.axis_index("seq"), lax.axis_index("head")
    z, k = lax.div(h, 2), lax.rem(h, 2)
    sibling = (s, h + 1 - 2 * k)
    half = shards // 2
    first, cross = s == 0, s == half
    gate = (s == half - 1) & (z == LINE - 1)
    entry = cross & (z == 0)
    has_next = (s < shards - 1) & (s != half - 1)
    has_prev = (s > 0) & (s != half)
    gate_int = gate.astype(jnp.int32)
    entry_int = entry.astype(jnp.int32)
    up = (s + gate_int, h + 2 - gate_int * 2 * LINE)
    down = (s - entry_int, h - 2 + entry_int * 2 * LINE)
    later, earlier = (s + 1, h), (s - 1, h)

    def exists(j):
        return s * LINE + z >= j

    def goes_next(j):
        return has_next & exists(j) if j <= LINE else None

    def goes_up(j):
        if j > SLOTS - 1:
            return None
        chain = gate | (cross & (z < LINE - 1))
        return chain | ((z < LINE - 1) & (z >= j)) if j < LINE else chain

    def goes_down(j):
        if j < 2 or j > LINE:
            return None
        return (z > 0) & (z < j) & jnp.logical_not(cross | first)

    def comes_up(j):
        return (z >= j) | cross

    def comes_down(j):
        return (z < j) & jnp.logical_not(cross | first)

    def slot(g, j):
        return kv.at[g, :, pl.ds((SLOTS - j) * block, block), :]

    def remote(src, dst, send, recv, device):
        return pltpu.make_async_remote_copy(
            src_ref=src, dst_ref=dst, send_sem=send, recv_sem=recv,
            device_id=device, device_id_type=MESH,
        )

    def when(condition, work):
        if condition is not None:
            pl.when(condition)(work)

    def columns(core, g, width):
        start = (core * groups + g) * width
        return pl.ds(pl.multiple_of(start, HEAD_SIZE), width)

    mine = pl.ds(pl.multiple_of(k * rows, 16), rows)
    theirs = pl.ds(pl.multiple_of((1 - k) * rows, 16), rows)
    mine_tail = pl.ds(pl.multiple_of(SLOTS * block + k * rows, 16), rows)

    def in_place(index, g):
        return (
            lambda: qb.at[g, mine, :], lambda: cb.at[g, mine, :],
            lambda: kv.at[g, 0, mine_tail, :], lambda: kv.at[g, 1, mine_tail, :],
        )[index]()

    def in_copies(index, g):
        source = (q_ref, c_ref, k_ref, v_ref)[index]
        width = wide if index < 2 else HEAD_SIZE
        local = pltpu.make_async_copy(
            source.at[:, columns(k, g, width)], in_place(index, g), x_local.at[g, index]
        )
        over = remote(
            source.at[:, columns(1 - k, g, width)], in_place(index, g),
            x_send.at[g, index], x_recv.at[g, index], sibling,
        )
        return local, over

    def start_in(index, g):
        local, over = in_copies(index, g)
        over.start()
        local.start()

    def wait_in(index, g):
        local, over = in_copies(index, g)
        local.wait()
        over.wait()

    def out_copies(index, g):
        target = (out_ref, dq_ref, dk_ref, dv_ref)[index]
        width = wide if index < 2 else HEAD_SIZE

        def part(which):
            if index < 2:
                return (ob, gb)[index].at[g, which, :]
            return stage.at[g, 0, index - 2, which, :]

        place = target.at[:, columns(k, g, width)]
        local = pltpu.make_async_copy(part(mine), place, o_local.at[g, index])
        over = remote(part(theirs), place, o_send.at[g, index], o_recv.at[g, index], sibling)
        return local, over

    def start_out(index, g):
        local, over = out_copies(index, g)
        over.start()
        local.start()

    def wait_out(index, g):
        local, over = out_copies(index, g)
        local.wait()
        over.wait()

    def next_copy(g, j):
        return remote(
            slot(g, j), slot(g, j + LINE), send_next.at[g, j], slot_recv.at[g, j + LINE], later
        )

    def up_copy(g, j):
        return remote(slot(g, j), slot(g, j + 1), send_up.at[g, j], slot_recv.at[g, j + 1], up)

    def down_copy(g, j):
        return remote(
            slot(g, j), slot(g, j - 1), send_down.at[g, j], slot_recv.at[g, j - 1], down
        )

    def forward(g, j):
        when(goes_next(j), lambda: next_copy(g, j).start())
        when(goes_up(j), lambda: up_copy(g, j).start())
        when(goes_down(j), lambda: down_copy(g, j).start())

    def relay(g, j, condition):
        def work():
            remote(
                slot(g, j), slot(g, j), send_next.at[g, 0], slot_recv.at[g, j], sibling
            ).wait_recv()
            forward(g, j)

        when(condition, work)

    def each(work):
        def body(g, _):
            work(g)
            return 0

        lax.fori_loop(0, groups, body, 0)

    def gather():
        steps = [(1, comes_up(1)), (4, exists(4)), (2, comes_up(2)), (3, comes_down(3))]
        steps += [(3, comes_up(3)), (2, comes_down(2)), (1, comes_down(1))]
        steps += [(j, exists(j)) for j in range(LINE + 1, SLOTS + 1)]
        for j, condition in steps:
            each(lambda g: relay(g, j, condition))

    def own(g):
        wait_in(2, g)
        wait_in(3, g)
        forward(g, 0)

    def span(j):
        return pl.ds((SLOTS - j) * block, block)

    def add(g, j, source, index, sem):
        remote(source.at[g, index], source.at[g, index], grad_send.at[g, 0], sem, sibling).wait_recv()
        acc[g, :, span(j), :] += source[g, index].astype(jnp.float32)

    def give(g, j, place, sem, device):
        return remote(stage.at[g, j], place, grad_send.at[g, j], sem, device)

    def to_down(g, j):
        return give(g, j, from_up.at[g, j - 1], up_recv.at[g, j - 1], down)

    def to_up(g, j):
        return give(g, j, from_down.at[g, j - 1], down_recv.at[g, j - 1], up)

    def to_earlier(g, j):
        return give(g, j, from_next.at[g, j - LINE], next_recv.at[g, j - LINE], earlier)

    def send_back(g, j, action):
        if j < LINE:
            pl.when(comes_up(j))(lambda: action(to_down(g, j)))
            pl.when(comes_down(j))(lambda: action(to_up(g, j)))
        else:
            pl.when(cross)(lambda: action(to_down(g, j)))
            pl.when(has_prev & exists(j))(lambda: action(to_earlier(g, j)))

    def give_back(g, j, condition):
        def work():
            when(goes_next(j), lambda: add(g, j, from_next, j, next_recv.at[g, j]))
            when(goes_up(j), lambda: add(g, j, from_up, j, up_recv.at[g, j]))
            when(goes_down(j), lambda: add(g, j, from_down, j - 2, down_recv.at[g, j - 2]))
            total = acc[g, :, span(j), :]
            if j == 0:
                stage[g, 0, 0] = (total[0] * SCALE).astype(jnp.bfloat16)
                stage[g, 0, 1] = total[1].astype(jnp.bfloat16)
                start_out(2, g)
                start_out(3, g)
            else:
                stage[g, j] = total.astype(jnp.bfloat16)
                send_back(g, j, lambda copy: copy.start())

        when(condition, work)

    def leaves(g):
        for j in range(SLOTS, LINE, -1):
            chained = goes_up(j)
            free = exists(j) if chained is None else exists(j) & jnp.logical_not(chained)
            give_back(g, j, free)

    def reduce():
        steps = [(j, goes_up(j)) for j in range(SLOTS - 1, LINE, -1)]
        steps += [(j, comes_down(j)) for j in range(1, LINE)] + [(LINE, exists(LINE))]
        steps += [(j, comes_up(j)) for j in range(LINE - 1, 0, -1)] + [(0, s >= 0)]
        for j, condition in steps:
            each(lambda g: give_back(g, j, condition))

    def gather_rows(g):
        wait_in(0, g)
        wait_in(1, g)
        for r in range(repeat):
            place = pl.ds(r * block, block)
            cols = pl.ds(r * HEAD_SIZE, HEAD_SIZE)
            qs[place, :] = qb[g, :, cols]
            cs[place, :] = cb[g, :, cols]

    def spread_rows(g):
        for r in range(repeat):
            place = pl.ds(r * block, block)
            cols = pl.ds(r * HEAD_SIZE, HEAD_SIZE)
            ob[g, :, cols] = os[place, :]
            gb[g, :, cols] = gs[place, :]
        start_out(0, g)
        start_out(1, g)

    def tile(g, n):
        place = pl.ds(n * TILE, TILE)
        query, cot = qs[place, :], cs[place, :]
        key, value = kv[g, 0], kv[g, 1]
        scores = dot(key, query, 1, 1) * (SCALE * math.log2(math.e)) + bias[:, place]
        top = jnp.max(scores, 0, keepdims=True)
        e = jnp.exp2(scores - top)
        inverse = 1.0 / jnp.sum(e, 0, keepdims=True)
        e_half = e.astype(jnp.bfloat16)
        cot_t = (cot.astype(jnp.float32).T * inverse).astype(jnp.bfloat16)
        out_t = dot(value, e_half, 0, 0) * inverse
        out_half = out_t.astype(jnp.bfloat16).astype(jnp.float32)
        delta = jnp.sum(out_half * cot_t.astype(jnp.float32), 0, keepdims=True)
        score_grad = (e * (dot(value, cot_t, 1, 0) - delta)).astype(jnp.bfloat16)
        query_grad_t = dot(key, score_grad, 0, 0) * SCALE
        acc[g, 0] += dot(score_grad, query, 1, 0)
        acc[g, 1] += dot(e_half, cot_t, 1, 1)
        os[place, :] = out_half.T.astype(jnp.bfloat16)
        gs[place, :] = query_grad_t.T.astype(jnp.bfloat16)

    barrier = pltpu.get_barrier_semaphore()

    def greet(device):
        pl.semaphore_signal(barrier, inc=1, device_id=device, device_id_type=MESH)

    has_up = (z < LINE - 1) | gate
    has_down = (z > 0) | entry
    greet(sibling)
    pl.when(has_up)(lambda: greet(up))
    pl.when(has_down)(lambda: greet(down))
    pl.when(has_next)(lambda: greet(later))
    pl.when(has_prev)(lambda: greet(earlier))
    friends = 1
    for there in (has_up, has_down, has_next, has_prev):
        friends = friends + there.astype(jnp.int32)
    pl.semaphore_wait(barrier, friends)

    def open_keys(g):
        start_in(2, g)
        start_in(3, g)

    def open_rows(g):
        start_in(0, g)
        start_in(1, g)

    def blanks(g):
        acc[g] = jnp.zeros((2, window, HEAD_SIZE), jnp.float32)
        for j in range(1, SLOTS + 1):

            def blank(j=j):
                kv[g, :, span(j), :] = jnp.zeros((2, block, HEAD_SIZE), jnp.bfloat16)

            pl.when(jnp.logical_not(exists(j)))(blank)

    each(open_keys)
    each(open_rows)
    each(own)
    each(blanks)
    place = lax.broadcasted_iota(jnp.int32, (window, stacked), 0)
    seen = (place >= bounds_ref[0:1, :]) & (place <= bounds_ref[1:2, :])
    bias[...] = jnp.where(seen, 0.0, HIDDEN)
    gather()

    def attend(g):
        gather_rows(g)

        def one(n, _):
            tile(g, n)
            return 0

        lax.fori_loop(0, stacked // TILE, one, 0)
        spread_rows(g)
        leaves(g)

    each(attend)
    reduce()

    def close(g, _):
        for index in range(4):
            wait_out(index, g)
        for j in range(SLOTS + 1):
            when(goes_next(j), lambda: next_copy(g, j).wait_send())
            when(goes_up(j), lambda: up_copy(g, j).wait_send())
            when(goes_down(j), lambda: down_copy(g, j).wait_send())
            if j > 0:
                send_back(g, j, lambda copy: copy.wait_send())
        return 0

    lax.fori_loop(0, groups, close, 0)


def shard(queries, keys, values, output_cotangent, doc_ids):
    shards = lax.axis_size("seq")
    rows = queries.shape[0]
    block = 2 * rows
    window = (SLOTS + 1) * block
    groups = keys.shape[1] // HEAD_SIZE // 2
    repeat = queries.shape[1] // keys.shape[1]
    stacked = repeat * block
    wide = repeat * HEAD_SIZE

    origin = (lax.axis_index("seq") * LINE + lax.axis_index("head") // 2) * block
    base = jnp.maximum(origin - SLOTS * block, 0)
    near = lax.dynamic_slice(doc_ids, (base,), (window,))
    here = lax.dynamic_slice(doc_ids, (origin,), (block,))
    begin = base + jnp.sum((near[None, :] < here[:, None]).astype(jnp.int32), 1)
    begin = begin - (origin - SLOTS * block)
    end = SLOTS * block + jnp.arange(block, dtype=jnp.int32)
    bounds = jnp.stack([jnp.tile(begin, repeat), jnp.tile(end, repeat)])

    bf16, f32 = jnp.bfloat16, jnp.float32
    any_spec = pl.BlockSpec(memory_space=pl.ANY)
    dma = pltpu.SemaphoreType.DMA
    pair = (2, block, HEAD_SIZE)
    return pl.pallas_call(
        functools.partial(kernel, shards, groups, repeat, rows),
        out_shape=(
            jax.ShapeDtypeStruct(queries.shape, bf16),
            jax.ShapeDtypeStruct(queries.shape, bf16),
            jax.ShapeDtypeStruct(keys.shape, bf16),
            jax.ShapeDtypeStruct(keys.shape, bf16),
        ),
        in_specs=[any_spec] * 4 + [pl.BlockSpec(memory_space=pltpu.VMEM)],
        out_specs=[any_spec] * 4,
        scratch_shapes=[
            pltpu.VMEM((groups, block, wide), bf16),
            pltpu.VMEM((groups, block, wide), bf16),
            pltpu.VMEM((groups, block, wide), bf16),
            pltpu.VMEM((groups, block, wide), bf16),
            pltpu.VMEM((groups, 2, window, HEAD_SIZE), bf16),
            pltpu.VMEM((window, stacked), f32),
            pltpu.VMEM((groups, 2, window, HEAD_SIZE), f32),
            pltpu.VMEM((stacked, HEAD_SIZE), bf16),
            pltpu.VMEM((stacked, HEAD_SIZE), bf16),
            pltpu.VMEM((stacked, HEAD_SIZE), bf16),
            pltpu.VMEM((stacked, HEAD_SIZE), bf16),
            pltpu.VMEM((groups, SLOTS + 1) + pair, bf16),
            pltpu.VMEM((groups, LINE + 1) + pair, bf16),
            pltpu.VMEM((groups, SLOTS) + pair, bf16),
            pltpu.VMEM((groups, LINE - 1) + pair, bf16),
            dma((groups, 4)), dma((groups, 4)), dma((groups, 4)),
            dma((groups, 4)), dma((groups, 4)), dma((groups, 4)),
            dma((groups, LINE + 1)), dma((groups, SLOTS)), dma((groups, LINE + 1)),
            dma((groups, SLOTS + 1)), dma((groups, SLOTS + 1)),
            dma((groups, LINE + 1)), dma((groups, SLOTS)), dma((groups, LINE - 1)),
        ],
        compiler_params=pltpu.CompilerParams(
            collective_id=0, has_side_effects=True, vmem_limit_bytes=56 * 1024 * 1024
        ),
    )(queries, keys, values, output_cotangent, bounds)


def solution(mesh):
    tokens = P(("seq", "head"), None)
    return jax.shard_map(
        shard,
        mesh=mesh,
        in_specs=(tokens, tokens, tokens, tokens, P()),
        out_specs=(tokens, tokens, tokens, tokens),
        check_vma=False,
    )
```

```python
import functools
import math

import jax
import jax.numpy as jnp
from jax import lax
from jax.experimental import pallas as pl
from jax.experimental.pallas import tpu as pltpu
from jax.sharding import PartitionSpec as P

MESH = pl.DeviceIdType.MESH
HEAD_SIZE = 128
SLOTS = 8
LINE = 4
SCALE = HEAD_SIZE**-0.5
TILE = 256
HIDDEN = -1e30


def dot(left, right, left_dim, right_dim):
    return lax.dot_general(
        left, right, (((left_dim,), (right_dim,)), ((), ())), preferred_element_type=jnp.float32
    )


def kernel(
    shards, groups, repeat, rows,
    q_ref, k_ref, v_ref, c_ref, bounds_ref,
    out_ref, dq_ref, dk_ref, dv_ref,
    qb, cb, ob, gb, kv, bias, acc, qs, cs, os, gs, stage, from_next, from_up, from_down,
    x_send, x_recv, x_local, o_send, o_recv, o_local,
    send_next, send_up, send_down, slot_recv, grad_send, next_recv, up_recv, down_recv,
):
    block = 2 * rows
    window = (SLOTS + 1) * block
    stacked = repeat * block
    wide = repeat * HEAD_SIZE
    s, h = lax.axis_index("seq"), lax.axis_index("head")
    z, k = lax.div(h, 2), lax.rem(h, 2)
    sibling = (s, h + 1 - 2 * k)
    first, cross, gate = s == 0, s == shards // 2, s == shards // 2 - 1
    has_next, has_prev = s < shards - 1, s > 0
    has_up, has_down = z < LINE - 1, z > 0
    up, down = (s, h + 2), (s, h - 2)
    later, earlier = (s + 1, h), (s - 1, h)

    def exists(j):
        return s * LINE + z >= j

    def comes_up(j):
        if j < LINE:
            return z >= j
        return cross & (z >= j - LINE) if LINE < j < SLOTS else None

    def comes_down(j):
        if j < LINE:
            return (z < j) & jnp.logical_not(first)
        return cross & (z < j - LINE) if LINE < j < SLOTS else None

    def comes_earlier(j):
        if j < LINE:
            return None
        return exists(j) if j % LINE == 0 else exists(j) & jnp.logical_not(cross)

    def goes_next(j):
        if j > LINE:
            return None
        there = has_next & exists(j)
        return there if j % LINE == 0 else there & jnp.logical_not(gate)

    def goes_up(j):
        if j < LINE:
            return has_up & (z >= j)
        return has_up & cross & (z >= j - LINE) if j < SLOTS - 1 else None

    def goes_down(j):
        if 2 <= j <= LINE:
            return has_down & (z < j) & jnp.logical_not(first)
        return has_down & cross & (z < j - LINE) if j >= LINE + 2 else None

    def inner_only(j, condition):
        chained = [c for c in (goes_up(j), goes_down(j)) if c is not None]
        chained = functools.reduce(lambda a, b: a | b, chained)
        return chained if condition is None else condition & chained

    def slot(g, j):
        return kv.at[g, :, pl.ds((SLOTS - j) * block, block), :]

    def remote(src, dst, send, recv, device):
        return pltpu.make_async_remote_copy(
            src_ref=src, dst_ref=dst, send_sem=send, recv_sem=recv,
            device_id=device, device_id_type=MESH,
        )

    def when(condition, work):
        if condition is not None:
            pl.when(condition)(work)

    def columns(core, g, width):
        start = (core * groups + g) * width
        return pl.ds(pl.multiple_of(start, HEAD_SIZE), width)

    mine = pl.ds(pl.multiple_of(k * rows, 16), rows)
    theirs = pl.ds(pl.multiple_of((1 - k) * rows, 16), rows)
    mine_tail = pl.ds(pl.multiple_of(SLOTS * block + k * rows, 16), rows)

    def in_place(index, g):
        return (
            lambda: qb.at[g, mine, :], lambda: cb.at[g, mine, :],
            lambda: kv.at[g, 0, mine_tail, :], lambda: kv.at[g, 1, mine_tail, :],
        )[index]()

    def in_copies(index, g):
        source = (q_ref, c_ref, k_ref, v_ref)[index]
        width = wide if index < 2 else HEAD_SIZE
        local = pltpu.make_async_copy(
            source.at[:, columns(k, g, width)], in_place(index, g), x_local.at[g, index]
        )
        over = remote(
            source.at[:, columns(1 - k, g, width)], in_place(index, g),
            x_send.at[g, index], x_recv.at[g, index], sibling,
        )
        return local, over

    def start_in(index, g):
        local, over = in_copies(index, g)
        over.start()
        local.start()

    def wait_in(index, g):
        local, over = in_copies(index, g)
        local.wait()
        over.wait()

    def out_copies(index, g):
        target = (out_ref, dq_ref, dk_ref, dv_ref)[index]
        width = wide if index < 2 else HEAD_SIZE

        def part(which):
            if index < 2:
                return (ob, gb)[index].at[g, which, :]
            return stage.at[g, 0, index - 2, which, :]

        place = target.at[:, columns(k, g, width)]
        local = pltpu.make_async_copy(part(mine), place, o_local.at[g, index])
        over = remote(part(theirs), place, o_send.at[g, index], o_recv.at[g, index], sibling)
        return local, over

    def start_out(index, g):
        local, over = out_copies(index, g)
        over.start()
        local.start()

    def wait_out(index, g):
        local, over = out_copies(index, g)
        local.wait()
        over.wait()

    def next_copy(g, j):
        return remote(
            slot(g, j), slot(g, j + LINE), send_next.at[g, j], slot_recv.at[g, j + LINE], later
        )

    def up_copy(g, j):
        return remote(slot(g, j), slot(g, j + 1), send_up.at[g, j], slot_recv.at[g, j + 1], up)

    def down_copy(g, j):
        return remote(
            slot(g, j), slot(g, j - 1), send_down.at[g, j], slot_recv.at[g, j - 1], down
        )

    def forward(g, j):
        when(goes_next(j), lambda: next_copy(g, j).start())
        when(goes_up(j), lambda: up_copy(g, j).start())
        when(goes_down(j), lambda: down_copy(g, j).start())

    def relay(g, j, condition):
        def work():
            remote(
                slot(g, j), slot(g, j), send_next.at[g, 0], slot_recv.at[g, j], sibling
            ).wait_recv()
            forward(g, j)

        when(condition, work)

    def each(work, begin=0, count=groups):
        def body(i, _):
            work(begin + i)
            return 0

        lax.fori_loop(0, count, body, 0)

    ways_out = [
        [(1, comes_up(1)), (4, comes_earlier(4)), (8, comes_earlier(8))],
        [(2, comes_up(2)), (3, comes_down(3)), (5, comes_up(5)), (7, comes_down(7))],
        [(3, comes_up(3)), (2, comes_down(2)), (6, comes_up(6)), (6, comes_down(6))],
        [(1, comes_down(1)), (7, comes_up(7)), (5, comes_down(5))],
        [(5, comes_earlier(5)), (6, comes_earlier(6))],
        [(7, comes_earlier(7))],
    ]

    def own(g):
        wait_in(2, g)
        wait_in(3, g)
        forward(g, 0)

    def span(j):
        return pl.ds((SLOTS - j) * block, block)

    def add(g, j, source, index, sem):
        remote(source.at[g, index], source.at[g, index], grad_send.at[g, 0], sem, sibling).wait_recv()
        acc[g, :, span(j), :] += source[g, index].astype(jnp.float32)

    def give(g, j, place, sem, device):
        return remote(stage.at[g, j], place, grad_send.at[g, j], sem, device)

    def to_down(g, j):
        return give(g, j, from_up.at[g, j - 1], up_recv.at[g, j - 1], down)

    def to_up(g, j):
        return give(g, j, from_down.at[g, j - 1], down_recv.at[g, j - 1], up)

    def to_earlier(g, j):
        return give(g, j, from_next.at[g, j - LINE], next_recv.at[g, j - LINE], earlier)

    def send_back(g, j, action):
        when(comes_up(j), lambda: action(to_down(g, j)))
        when(comes_down(j), lambda: action(to_up(g, j)))
        when(comes_earlier(j), lambda: action(to_earlier(g, j)))

    def give_back(g, j, condition):
        def work():
            when(goes_next(j), lambda: add(g, j, from_next, j, next_recv.at[g, j]))
            when(goes_up(j), lambda: add(g, j, from_up, j, up_recv.at[g, j]))
            when(goes_down(j), lambda: add(g, j, from_down, j - 2, down_recv.at[g, j - 2]))
            total = acc[g, :, span(j), :]
            if j == 0:
                stage[g, 0, 0] = (total[0] * SCALE).astype(jnp.bfloat16)
                stage[g, 0, 1] = total[1].astype(jnp.bfloat16)
                start_out(2, g)
                start_out(3, g)
            else:
                stage[g, j] = total.astype(jnp.bfloat16)
                send_back(g, j, lambda copy: copy.start())

        when(condition, work)

    def leaves(g):
        for j in range(SLOTS, LINE, -1):
            give_back(g, j, exists(j) & jnp.logical_not(inner_only(j, None)))

    ways_back = [
        [(1, comes_down(1)), (3, comes_up(3))]
        + [(j, inner_only(j, comes_down(j))) for j in (5, 6, 7)],
        [(2, comes_down(2)), (2, comes_up(2))]
        + [(8, inner_only(8, None)), (7, inner_only(7, comes_up(7)))],
        [(3, comes_down(3)), (1, comes_up(1)), (6, inner_only(6, comes_up(6)))],
        [(5, inner_only(5, comes_up(5)))],
        [(4, comes_earlier(4))],
        [(0, s >= 0)],
    ]

    def gather_rows(g):
        wait_in(0, g)
        wait_in(1, g)
        for r in range(repeat):
            place = pl.ds(r * block, block)
            cols = pl.ds(r * HEAD_SIZE, HEAD_SIZE)
            qs[place, :] = qb[g, :, cols]
            cs[place, :] = cb[g, :, cols]

    def spread_rows(g):
        for r in range(repeat):
            place = pl.ds(r * block, block)
            cols = pl.ds(r * HEAD_SIZE, HEAD_SIZE)
            ob[g, :, cols] = os[place, :]
            gb[g, :, cols] = gs[place, :]
        start_out(0, g)
        start_out(1, g)

    def tile(g, n):
        place = pl.ds(n * TILE, TILE)
        query, cot = qs[place, :], cs[place, :]
        key, value = kv[g, 0], kv[g, 1]
        scores = dot(key, query, 1, 1) * (SCALE * math.log2(math.e)) + bias[:, place]
        top = jnp.max(scores, 0, keepdims=True)
        e = jnp.exp2(scores - top)
        inverse = 1.0 / jnp.sum(e, 0, keepdims=True)
        e_half = e.astype(jnp.bfloat16)
        cot_t = (cot.astype(jnp.float32).T * inverse).astype(jnp.bfloat16)
        out_t = dot(value, e_half, 0, 0) * inverse
        out_half = out_t.astype(jnp.bfloat16).astype(jnp.float32)
        delta = jnp.sum(out_half * cot_t.astype(jnp.float32), 0, keepdims=True)
        score_grad = (e * (dot(value, cot_t, 1, 0) - delta)).astype(jnp.bfloat16)
        query_grad_t = dot(key, score_grad, 0, 0) * SCALE
        acc[g, 0] += dot(score_grad, query, 1, 0)
        acc[g, 1] += dot(e_half, cot_t, 1, 1)
        os[place, :] = out_half.T.astype(jnp.bfloat16)
        gs[place, :] = query_grad_t.T.astype(jnp.bfloat16)

    barrier = pltpu.get_barrier_semaphore()

    def greet(device):
        pl.semaphore_signal(barrier, inc=1, device_id=device, device_id_type=MESH)

    greet(sibling)
    pl.when(has_up)(lambda: greet(up))
    pl.when(has_down)(lambda: greet(down))
    pl.when(has_next)(lambda: greet(later))
    pl.when(has_prev)(lambda: greet(earlier))
    friends = 1
    for there in (has_up, has_down, has_next, has_prev):
        friends = friends + there.astype(jnp.int32)
    pl.semaphore_wait(barrier, friends)

    def open_keys(g):
        start_in(2, g)
        start_in(3, g)

    def open_rows(g):
        start_in(0, g)
        start_in(1, g)

    def blanks(g):
        acc[g] = jnp.zeros((2, window, HEAD_SIZE), jnp.float32)
        for j in range(1, SLOTS + 1):

            def blank(j=j):
                kv[g, :, span(j), :] = jnp.zeros((2, block, HEAD_SIZE), jnp.bfloat16)

            pl.when(jnp.logical_not(exists(j)))(blank)

    each(open_keys)
    each(open_rows)
    each(own, 0, groups // 2)
    each(blanks)
    place = lax.broadcasted_iota(jnp.int32, (window, stacked), 0)
    seen = (place >= bounds_ref[0:1, :]) & (place <= bounds_ref[1:2, :])
    bias[...] = jnp.where(seen, 0.0, HIDDEN)
    part = groups // 2
    tiles = stacked // TILE
    parts = part * tiles

    def step(i, _):
        r, t = lax.div(i, parts), lax.rem(i, parts)
        working = (r >= 1) & (r <= 2)
        n = lax.rem(t, tiles)
        g = (r - 1) * part + lax.div(t, tiles)

        @pl.when(working & (n == 0))
        def _():
            gather_rows(g)

        @pl.when(working)
        def _():
            tile(g, n)

        @pl.when(working & (n == tiles - 1))
        def _():
            spread_rows(g)
            leaves(g)

        for place, steps in enumerate(ways_out):

            @pl.when((r < 2) & (t == place))
            def _(steps=steps):
                for j, condition in steps:
                    each(lambda g: relay(g, j, condition), r * part, part)

        @pl.when(i == 1)
        def _():
            each(own, part, part)

        for place, steps in enumerate(ways_back):

            @pl.when((r >= 2) & (t == place))
            def _(steps=steps):
                for j, condition in steps:
                    each(lambda g: give_back(g, j, condition), (r - 2) * part, part)

        return 0

    lax.fori_loop(0, 4 * parts, step, 0)

    def close(g, _):
        for index in range(4):
            wait_out(index, g)
        for j in range(SLOTS + 1):
            when(goes_next(j), lambda: next_copy(g, j).wait_send())
            when(goes_up(j), lambda: up_copy(g, j).wait_send())
            when(goes_down(j), lambda: down_copy(g, j).wait_send())
            if j > 0:
                send_back(g, j, lambda copy: copy.wait_send())
        return 0

    lax.fori_loop(0, groups, close, 0)


def shard(queries, keys, values, output_cotangent, doc_ids):
    shards = lax.axis_size("seq")
    rows = queries.shape[0]
    block = 2 * rows
    window = (SLOTS + 1) * block
    groups = keys.shape[1] // HEAD_SIZE // 2
    repeat = queries.shape[1] // keys.shape[1]
    stacked = repeat * block
    wide = repeat * HEAD_SIZE

    origin = (lax.axis_index("seq") * LINE + lax.axis_index("head") // 2) * block
    base = jnp.maximum(origin - SLOTS * block, 0)
    near = lax.dynamic_slice(doc_ids, (base,), (window,))
    here = lax.dynamic_slice(doc_ids, (origin,), (block,))
    begin = base + jnp.sum((near[None, :] < here[:, None]).astype(jnp.int32), 1)
    begin = begin - (origin - SLOTS * block)
    end = SLOTS * block + jnp.arange(block, dtype=jnp.int32)
    bounds = jnp.stack([jnp.tile(begin, repeat), jnp.tile(end, repeat)])

    bf16, f32 = jnp.bfloat16, jnp.float32
    any_spec = pl.BlockSpec(memory_space=pl.ANY)
    dma = pltpu.SemaphoreType.DMA
    pair = (2, block, HEAD_SIZE)
    return pl.pallas_call(
        functools.partial(kernel, shards, groups, repeat, rows),
        out_shape=(
            jax.ShapeDtypeStruct(queries.shape, bf16),
            jax.ShapeDtypeStruct(queries.shape, bf16),
            jax.ShapeDtypeStruct(keys.shape, bf16),
            jax.ShapeDtypeStruct(keys.shape, bf16),
        ),
        in_specs=[any_spec] * 4 + [pl.BlockSpec(memory_space=pltpu.VMEM)],
        out_specs=[any_spec] * 4,
        scratch_shapes=[
            pltpu.VMEM((groups, block, wide), bf16),
            pltpu.VMEM((groups, block, wide), bf16),
            pltpu.VMEM((groups, block, wide), bf16),
            pltpu.VMEM((groups, block, wide), bf16),
            pltpu.VMEM((groups, 2, window, HEAD_SIZE), bf16),
            pltpu.VMEM((window, stacked), f32),
            pltpu.VMEM((groups, 2, window, HEAD_SIZE), f32),
            pltpu.VMEM((stacked, HEAD_SIZE), bf16),
            pltpu.VMEM((stacked, HEAD_SIZE), bf16),
            pltpu.VMEM((stacked, HEAD_SIZE), bf16),
            pltpu.VMEM((stacked, HEAD_SIZE), bf16),
            pltpu.VMEM((groups, SLOTS + 1) + pair, bf16),
            pltpu.VMEM((groups, LINE + 1) + pair, bf16),
            pltpu.VMEM((groups, SLOTS - 1) + pair, bf16),
            pltpu.VMEM((groups, SLOTS - 1) + pair, bf16),
            dma((groups, 4)), dma((groups, 4)), dma((groups, 4)),
            dma((groups, 4)), dma((groups, 4)), dma((groups, 4)),
            dma((groups, LINE + 1)), dma((groups, SLOTS - 1)), dma((groups, SLOTS + 1)),
            dma((groups, SLOTS + 1)), dma((groups, SLOTS + 1)),
            dma((groups, LINE + 1)), dma((groups, SLOTS - 1)), dma((groups, SLOTS - 1)),
        ],
        compiler_params=pltpu.CompilerParams(
            collective_id=0, has_side_effects=True, vmem_limit_bytes=56 * 1024 * 1024
        ),
    )(queries, keys, values, output_cotangent, bounds)


def solution(mesh):
    tokens = P(("seq", "head"), None)
    return jax.shard_map(
        shard,
        mesh=mesh,
        in_specs=(tokens, tokens, tokens, tokens, P()),
        out_specs=(tokens, tokens, tokens, tokens),
        check_vma=False,
    )
```

```python
import functools
import math

import jax
import jax.numpy as jnp
from jax import lax
from jax.experimental import pallas as pl
from jax.experimental.pallas import tpu as pltpu
from jax.sharding import PartitionSpec as P

MESH = pl.DeviceIdType.MESH
HEAD_SIZE = 128
SLOTS = 8
LINE = 4
SCALE = HEAD_SIZE**-0.5
TILE = 256
HIDDEN = -1e30


def dot(left, right, left_dim, right_dim):
    return lax.dot_general(
        left, right, (((left_dim,), (right_dim,)), ((), ())), preferred_element_type=jnp.float32
    )


def hand_on(*refs):
    copies = [pltpu.make_async_copy(refs[i], refs[4 + i], refs[8].at[i]) for i in range(4)]
    for copy in copies:
        copy.start()
    for copy in copies:
        copy.wait()


def kernel(
    shards, groups, repeat, rows,
    q_ref, k_ref, v_ref, c_ref, bounds_ref,
    out_ref, dq_ref, dk_ref, dv_ref,
    qb, cb, ob, gb, kv, bias, acc, qs, cs, os, gs, stage, from_next, from_line,
    key_t, value_t, e_all, grad_all, cot_n,
    x_send, x_recv, x_local, o_send, o_recv, o_local,
    send_next, send_line, slot_recv, grad_send, next_recv, line_recv,
):
    block = 2 * rows
    window = (SLOTS + 1) * block
    stacked = repeat * block
    wide = repeat * HEAD_SIZE
    s, h = lax.axis_index("seq"), lax.axis_index("head")
    z, k = lax.div(h, 2), lax.rem(h, 2)
    sibling = (s, h + 1 - 2 * k)
    first, cross, gate = s == 0, s == shards // 2, s == shards // 2 - 1
    has_next, has_prev = s < shards - 1, s > 0
    later, earlier = (s + 1, h), (s - 1, h)

    def exists(j):
        return s * LINE + z >= j

    def goes_next(j):
        if j > LINE:
            return None
        there = has_next & exists(j)
        return there if j % LINE == 0 else there & jnp.logical_not(gate)

    def comes_earlier(j):
        if j < LINE:
            return None
        return exists(j) if j % LINE == 0 else exists(j) & jnp.logical_not(cross)

    kinds = ((0, 1), (LINE, -1), (LINE, 1), (SLOTS, -1))
    allowed = (s >= 0, jnp.logical_not(first), cross, cross)

    def there(kind, distance):
        place = z + kinds[kind][1] * distance
        return allowed[kind] & (place >= 0) & (place < LINE)

    def back(kind, distance):
        place = z - kinds[kind][1] * distance
        return allowed[kind] & (place >= 0) & (place < LINE)

    def in_line(kind, distance):
        return (s, h + 2 * kinds[kind][1] * distance)

    def in_line_back(kind, distance):
        return (s, h - 2 * kinds[kind][1] * distance)

    def landing(kind, distance):
        return kinds[kind][0] + kinds[kind][1] * distance

    ways = [(kind, distance) for kind in range(4) for distance in range(1, LINE)]

    def slot(g, j):
        return kv.at[g, :, pl.ds((SLOTS - j) * block, block), :]

    def remote(src, dst, send, recv, device):
        return pltpu.make_async_remote_copy(
            src_ref=src, dst_ref=dst, send_sem=send, recv_sem=recv,
            device_id=device, device_id_type=MESH,
        )

    def when(condition, work):
        if condition is not None:
            pl.when(condition)(work)

    def columns(core, g, width):
        start = (core * groups + g) * width
        return pl.ds(pl.multiple_of(start, HEAD_SIZE), width)

    mine = pl.ds(pl.multiple_of(k * rows, 16), rows)
    theirs = pl.ds(pl.multiple_of((1 - k) * rows, 16), rows)
    mine_tail = pl.ds(pl.multiple_of(SLOTS * block + k * rows, 16), rows)

    def in_place(index, g):
        return (
            lambda: qb.at[g, mine, :], lambda: cb.at[g, mine, :],
            lambda: kv.at[g, 0, mine_tail, :], lambda: kv.at[g, 1, mine_tail, :],
        )[index]()

    def in_copies(index, g):
        source = (q_ref, c_ref, k_ref, v_ref)[index]
        width = wide if index < 2 else HEAD_SIZE
        local = pltpu.make_async_copy(
            source.at[:, columns(k, g, width)], in_place(index, g), x_local.at[g, index]
        )
        over = remote(
            source.at[:, columns(1 - k, g, width)], in_place(index, g),
            x_send.at[g, index], x_recv.at[g, index], sibling,
        )
        return local, over

    def start_in(index, g):
        local, over = in_copies(index, g)
        over.start()
        local.start()

    def wait_in(index, g):
        local, over = in_copies(index, g)
        local.wait()
        over.wait()

    def out_copies(index, g):
        target = (out_ref, dq_ref, dk_ref, dv_ref)[index]
        width = wide if index < 2 else HEAD_SIZE

        def part(which):
            if index < 2:
                return (ob, gb)[index].at[g, which, :]
            return stage.at[g, 0, index - 2, which, :]

        place = target.at[:, columns(k, g, width)]
        local = pltpu.make_async_copy(part(mine), place, o_local.at[g, index])
        over = remote(part(theirs), place, o_send.at[g, index], o_recv.at[g, index], sibling)
        return local, over

    def start_out(index, g):
        local, over = out_copies(index, g)
        over.start()
        local.start()

    def wait_out(index, g):
        local, over = out_copies(index, g)
        local.wait()
        over.wait()

    def next_copy(g, j):
        return remote(
            slot(g, j), slot(g, j + LINE), send_next.at[g, j], slot_recv.at[g, j + LINE], later
        )

    def line_copy(g, kind, distance):
        to = landing(kind, distance)
        return remote(
            slot(g, kinds[kind][0]), slot(g, to), send_line.at[g, ways.index((kind, distance))],
            slot_recv.at[g, to], in_line(kind, distance),
        )

    def forward(g, j):
        for kind, distance in ways:
            if kinds[kind][0] == j:
                when(there(kind, distance), lambda: line_copy(g, kind, distance).start())
        when(goes_next(j), lambda: next_copy(g, j).start())

    def relay(g, j):
        def work():
            remote(
                slot(g, j), slot(g, j), send_next.at[g, 0], slot_recv.at[g, j], sibling
            ).wait_recv()
            forward(g, j)

        when(exists(j), work)

    part = groups // 2

    def each(work, begin=0, count=groups):
        def body(i, _):
            work(begin + i)
            return 0

        lax.fori_loop(0, count, body, 0)

    def out(begin, *slots):
        for j in slots:
            each(lambda g: relay(g, j), begin, part)

    def own(g):
        wait_in(2, g)
        wait_in(3, g)
        forward(g, 0)

    def span(j):
        return pl.ds((SLOTS - j) * block, block)

    def add(g, j, source, sem):
        remote(source, source, grad_send.at[g, 0], sem, sibling).wait_recv()
        acc[g, :, span(j), :] += source[...].astype(jnp.float32)

    def give(g, j, place, sem, device):
        return remote(stage.at[g, j], place, grad_send.at[g, j], sem, device)

    def send_back(g, j, action):
        for index, (kind, distance) in enumerate(ways):
            if landing(kind, distance) == j:
                when(
                    back(kind, distance),
                    lambda: action(
                        give(
                            g, j, from_line.at[g, index], line_recv.at[g, index],
                            in_line_back(kind, distance),
                        )
                    ),
                )
        when(
            comes_earlier(j),
            lambda: action(
                give(g, j, from_next.at[g, j - LINE], next_recv.at[g, j - LINE], earlier)
            ),
        )

    def give_back(g, j, condition):
        def work():
            for index, (kind, distance) in enumerate(ways):
                if kinds[kind][0] == j:
                    when(
                        there(kind, distance),
                        lambda: add(g, j, from_line.at[g, index], line_recv.at[g, index]),
                    )
            when(goes_next(j), lambda: add(g, j, from_next.at[g, j], next_recv.at[g, j]))
            total = acc[g, :, span(j), :]
            if j == 0:
                stage[g, 0, 0] = (total[0] * SCALE).astype(jnp.bfloat16)
                stage[g, 0, 1] = total[1].astype(jnp.bfloat16)
                start_out(2, g)
                start_out(3, g)
            else:
                stage[g, j] = total.astype(jnp.bfloat16)
                send_back(g, j, lambda copy: copy.start())

        when(condition, work)

    chained = cross & (z > 0)

    def leaves(g):
        for j in range(LINE + 1, SLOTS):
            give_back(g, j, exists(j))
        give_back(g, SLOTS, exists(SLOTS) & jnp.logical_not(chained))

    def home(begin, *slots):
        for j in slots:
            there_is = chained if j == SLOTS else exists(j)
            each(lambda g: give_back(g, j, there_is), begin, part)

    def gather_rows(g):
        wait_in(0, g)
        wait_in(1, g)
        for r in range(repeat):
            place = pl.ds(r * block, block)
            cols = pl.ds(r * HEAD_SIZE, HEAD_SIZE)
            qs[place, :] = qb[g, :, cols]
            cs[place, :] = cb[g, :, cols]

    def spread_rows(g):
        for r in range(repeat):
            place = pl.ds(r * block, block)
            cols = pl.ds(r * HEAD_SIZE, HEAD_SIZE)
            ob[g, :, cols] = os[place, :]
            gb[g, :, cols] = gs[place, :]
        start_out(0, g)
        start_out(1, g)

    def attend(g):
        gather_rows(g)
        key, value = kv[g, 0], kv[g, 1]
        key_t[...] = key.T
        value_t[...] = value.T
        tiles = [pl.ds(n * TILE, TILE) for n in range(stacked // TILE)]

        def score(place):
            raw = dot(key, qs[place, :], 1, 1) * (SCALE * math.log2(math.e))
            return raw + bias[:, place]

        scores = score(tiles[0])
        for n, place in enumerate(tiles):
            later_scores = score(tiles[n + 1]) if n + 1 < len(tiles) else None
            top = jnp.max(scores, 0, keepdims=True)
            e = jnp.exp2(scores - top)
            inverse = 1.0 / jnp.sum(e, 0, keepdims=True)
            e_half = e.astype(jnp.bfloat16)
            e_all[:, place] = e_half
            cot_t = (cs[place, :].astype(jnp.float32).T * inverse).astype(jnp.bfloat16)
            cot_n[place, :] = cot_t.astype(jnp.float32).T.astype(jnp.bfloat16)
            out_t = dot(value_t[...], e_half, 1, 0) * inverse
            out_half = out_t.astype(jnp.bfloat16).astype(jnp.float32)
            delta = jnp.sum(out_half * cot_t.astype(jnp.float32), 0, keepdims=True)
            score_grad = (e * (dot(value, cot_t, 1, 0) - delta)).astype(jnp.bfloat16)
            grad_all[:, place] = score_grad
            query_grad_t = dot(key_t[...], score_grad, 1, 0) * SCALE
            os[place, :] = out_half.T.astype(jnp.bfloat16)
            gs[place, :] = query_grad_t.T.astype(jnp.bfloat16)
            scores = later_scores
        acc[g, 1] = dot(e_all[...], cot_n[...], 1, 0)
        acc[g, 0] = dot(grad_all[...], qs[...], 1, 0)
        spread_rows(g)

    barrier = pltpu.get_barrier_semaphore()

    def greet(device):
        pl.semaphore_signal(barrier, inc=1, device_id=device, device_id_type=MESH)

    greet(sibling)
    friends = 1
    neighbours = [(has_next, later), (has_prev, earlier)]
    for distance in range(1, LINE):
        neighbours.append((z + distance < LINE, (s, h + 2 * distance)))
        neighbours.append((z >= distance, (s, h - 2 * distance)))
    for near, device in neighbours:
        when(near, lambda: greet(device))
        friends = friends + near.astype(jnp.int32)
    pl.semaphore_wait(barrier, friends)

    def open_keys(g):
        start_in(2, g)
        start_in(3, g)

    def open_rows(g):
        start_in(0, g)
        start_in(1, g)

    def blanks(g):
        for j in range(1, SLOTS + 1):

            def blank(j=j):
                kv[g, :, span(j), :] = jnp.zeros((2, block, HEAD_SIZE), jnp.bfloat16)

            pl.when(jnp.logical_not(exists(j)))(blank)

    each(open_keys)
    each(open_rows)
    each(own, 0, part)
    each(blanks)
    place = lax.broadcasted_iota(jnp.int32, (window, stacked), 0)
    seen = (place >= bounds_ref[0:1, :]) & (place <= bounds_ref[1:2, :])
    bias[...] = jnp.where(seen, 0.0, HIDDEN)
    out(0, 4)
    each(own, part, part)
    out(0, 1, 8, 2, 3, 5, 6, 7)
    out(part, 4, 1)

    def step(g, _):
        attend(g)
        leaves(g)

        @pl.when(g == 0)
        def _():
            out(part, 8, 2, 3)

        @pl.when(g == part - 1)
        def _():
            out(part, 5, 6, 7)

        @pl.when(g == part)
        def _():
            home(0, 1, 2, 3)

        return 0

    lax.fori_loop(0, groups, step, 0)
    home(0, 8, 4, 0)
    home(part, 1, 2, 3, 8, 4, 0)

    def close(g, _):
        for index in range(4):
            wait_out(index, g)
        for j in range(SLOTS + 1):
            when(goes_next(j), lambda: next_copy(g, j).wait_send())
            if j > 0:
                send_back(g, j, lambda copy: copy.wait_send())
        for kind, distance in ways:
            when(there(kind, distance), lambda: line_copy(g, kind, distance).wait_send())
        return 0

    lax.fori_loop(0, groups, close, 0)


def shard(queries, keys, values, output_cotangent, doc_ids):
    shards = lax.axis_size("seq")
    rows = queries.shape[0]
    block = 2 * rows
    window = (SLOTS + 1) * block
    groups = keys.shape[1] // HEAD_SIZE // 2
    repeat = queries.shape[1] // keys.shape[1]
    stacked = repeat * block
    wide = repeat * HEAD_SIZE

    origin = (lax.axis_index("seq") * LINE + lax.axis_index("head") // 2) * block
    base = jnp.maximum(origin - SLOTS * block, 0)
    near = lax.dynamic_slice(doc_ids, (base,), (window,))
    here = lax.dynamic_slice(doc_ids, (origin,), (block,))
    begin = base + jnp.sum((near[None, :] < here[:, None]).astype(jnp.int32), 1)
    begin = begin - (origin - SLOTS * block)
    end = SLOTS * block + jnp.arange(block, dtype=jnp.int32)
    bounds = jnp.stack([jnp.tile(begin, repeat), jnp.tile(end, repeat)])

    bf16, f32 = jnp.bfloat16, jnp.float32
    any_spec = pl.BlockSpec(memory_space=pl.ANY)
    dma = pltpu.SemaphoreType.DMA
    pair = (2, block, HEAD_SIZE)
    results = pl.pallas_call(
        functools.partial(kernel, shards, groups, repeat, rows),
        out_shape=(
            jax.ShapeDtypeStruct(queries.shape, bf16),
            jax.ShapeDtypeStruct(queries.shape, bf16),
            jax.ShapeDtypeStruct(keys.shape, bf16),
            jax.ShapeDtypeStruct(keys.shape, bf16),
        ),
        in_specs=[any_spec] * 4 + [pl.BlockSpec(memory_space=pltpu.VMEM)],
        out_specs=[any_spec] * 4,
        scratch_shapes=[
            pltpu.VMEM((groups, block, wide), bf16),
            pltpu.VMEM((groups, block, wide), bf16),
            pltpu.VMEM((groups, block, wide), bf16),
            pltpu.VMEM((groups, block, wide), bf16),
            pltpu.VMEM((groups, 2, window, HEAD_SIZE), bf16),
            pltpu.VMEM((window, stacked), f32),
            pltpu.VMEM((groups, 2, window, HEAD_SIZE), f32),
            pltpu.VMEM((stacked, HEAD_SIZE), bf16),
            pltpu.VMEM((stacked, HEAD_SIZE), bf16),
            pltpu.VMEM((stacked, HEAD_SIZE), bf16),
            pltpu.VMEM((stacked, HEAD_SIZE), bf16),
            pltpu.VMEM((groups, SLOTS + 1) + pair, bf16),
            pltpu.VMEM((groups, LINE + 1) + pair, bf16),
            pltpu.VMEM((groups, 4 * (LINE - 1)) + pair, bf16),
            pltpu.VMEM((HEAD_SIZE, window), bf16),
            pltpu.VMEM((HEAD_SIZE, window), bf16),
            pltpu.VMEM((window, stacked), bf16),
            pltpu.VMEM((window, stacked), bf16),
            pltpu.VMEM((stacked, HEAD_SIZE), bf16),
            dma((groups, 4)), dma((groups, 4)), dma((groups, 4)),
            dma((groups, 4)), dma((groups, 4)), dma((groups, 4)),
            dma((groups, LINE + 1)), dma((groups, 4 * (LINE - 1))), dma((groups, SLOTS + 1)),
            dma((groups, SLOTS + 1)), dma((groups, LINE + 1)), dma((groups, 4 * (LINE - 1))),
        ],
        compiler_params=pltpu.CompilerParams(
            collective_id=0, has_side_effects=True, vmem_limit_bytes=56 * 1024 * 1024
        ),
    )(queries, keys, values, output_cotangent, bounds)
    return pl.pallas_call(
        hand_on,
        out_shape=tuple(jax.ShapeDtypeStruct(r.shape, r.dtype) for r in results),
        in_specs=[any_spec] * 4,
        out_specs=[any_spec] * 4,
        scratch_shapes=[dma((4,))],
    )(*results)


def solution(mesh):
    tokens = P(("seq", "head"), None)
    return jax.shard_map(
        shard,
        mesh=mesh,
        in_specs=(tokens, tokens, tokens, tokens, P()),
        out_specs=(tokens, tokens, tokens, tokens),
        check_vma=False,
    )
```

```python
import functools
import math

import jax
import jax.numpy as jnp
from jax import lax
from jax.experimental import pallas as pl
from jax.experimental.pallas import tpu as pltpu
from jax.sharding import PartitionSpec as P

MESH = pl.DeviceIdType.MESH
HEAD_SIZE = 128
SLOTS = 8
LINE = 4
SCALE = HEAD_SIZE**-0.5
TILE = 256
HIDDEN = -1e30


def dot(left, right, left_dim, right_dim):
    return lax.dot_general(
        left, right, (((left_dim,), (right_dim,)), ((), ())), preferred_element_type=jnp.float32
    )


def hand_on(*refs):
    for i in range(4):
        refs[4 + i][...] = refs[i][...]


def kernel(
    shards, groups, repeat, rows,
    q_ref, k_ref, v_ref, c_ref, bounds_ref,
    out_ref, dq_ref, dk_ref, dv_ref,
    qb, cb, ob, gb, kv, bias, acc, qs, cs, os, gs, stage, from_next, from_line,
    key_t, value_t, e_all, grad_all, cot_n,
    x_send, x_recv, x_local, o_send, o_recv, o_local,
    send_next, send_line, slot_recv, grad_send, next_recv, line_recv,
):
    block = 2 * rows
    window = (SLOTS + 1) * block
    stacked = repeat * block
    wide = repeat * HEAD_SIZE
    s, h = lax.axis_index("seq"), lax.axis_index("head")
    z, k = lax.div(h, 2), lax.rem(h, 2)
    sibling = (s, h + 1 - 2 * k)
    first, cross, gate = s == 0, s == shards // 2, s == shards // 2 - 1
    has_next, has_prev = s < shards - 1, s > 0
    later, earlier = (s + 1, h), (s - 1, h)

    def exists(j):
        return s * LINE + z >= j

    def goes_next(j):
        if j > LINE:
            return None
        there = has_next & exists(j)
        return there if j % LINE == 0 else there & jnp.logical_not(gate)

    def comes_earlier(j):
        if j < LINE:
            return None
        return exists(j) if j % LINE == 0 else exists(j) & jnp.logical_not(cross)

    kinds = ((0, 1), (LINE, -1), (LINE, 1), (SLOTS, -1))
    allowed = (s >= 0, jnp.logical_not(first), cross, cross)

    def there(kind, distance):
        place = z + kinds[kind][1] * distance
        return allowed[kind] & (place >= 0) & (place < LINE)

    def back(kind, distance):
        place = z - kinds[kind][1] * distance
        return allowed[kind] & (place >= 0) & (place < LINE)

    def in_line(kind, distance):
        return (s, h + 2 * kinds[kind][1] * distance)

    def in_line_back(kind, distance):
        return (s, h - 2 * kinds[kind][1] * distance)

    def landing(kind, distance):
        return kinds[kind][0] + kinds[kind][1] * distance

    ways = [(kind, distance) for kind in range(4) for distance in range(1, LINE)]

    def slot(g, j):
        return kv.at[g, :, pl.ds((SLOTS - j) * block, block), :]

    def remote(src, dst, send, recv, device):
        return pltpu.make_async_remote_copy(
            src_ref=src, dst_ref=dst, send_sem=send, recv_sem=recv,
            device_id=device, device_id_type=MESH,
        )

    def when(condition, work):
        if condition is not None:
            pl.when(condition)(work)

    def columns(core, g, width):
        start = (core * groups + g) * width
        return pl.ds(pl.multiple_of(start, HEAD_SIZE), width)

    mine = pl.ds(pl.multiple_of(k * rows, 16), rows)
    theirs = pl.ds(pl.multiple_of((1 - k) * rows, 16), rows)
    mine_tail = pl.ds(pl.multiple_of(SLOTS * block + k * rows, 16), rows)

    def in_place(index, g):
        return (
            lambda: qb.at[g, mine, :], lambda: cb.at[g, mine, :],
            lambda: kv.at[g, 0, mine_tail, :], lambda: kv.at[g, 1, mine_tail, :],
        )[index]()

    def in_copies(index, g):
        source = (q_ref, c_ref, k_ref, v_ref)[index]
        width = wide if index < 2 else HEAD_SIZE
        local = pltpu.make_async_copy(
            source.at[:, columns(k, g, width)], in_place(index, g), x_local.at[g, index]
        )
        over = remote(
            source.at[:, columns(1 - k, g, width)], in_place(index, g),
            x_send.at[g, index], x_recv.at[g, index], sibling,
        )
        return local, over

    def start_in(index, g):
        local, over = in_copies(index, g)
        over.start()
        local.start()

    def wait_in(index, g):
        local, over = in_copies(index, g)
        local.wait()
        over.wait()

    def out_copies(index, g):
        target = (out_ref, dq_ref, dk_ref, dv_ref)[index]
        width = wide if index < 2 else HEAD_SIZE

        def part(which):
            if index < 2:
                return (ob, gb)[index].at[g, which, :]
            return stage.at[g, 0, index - 2, which, :]

        place = target.at[:, columns(k, g, width)]
        local = pltpu.make_async_copy(part(mine), place, o_local.at[g, index])
        over = remote(part(theirs), place, o_send.at[g, index], o_recv.at[g, index], sibling)
        return local, over

    def start_out(index, g):
        local, over = out_copies(index, g)
        over.start()
        local.start()

    def wait_out(index, g):
        local, over = out_copies(index, g)
        local.wait()
        over.wait()

    def next_copy(g, j):
        return remote(
            slot(g, j), slot(g, j + LINE), send_next.at[g, j], slot_recv.at[g, j + LINE], later
        )

    def line_copy(g, kind, distance):
        to = landing(kind, distance)
        return remote(
            slot(g, kinds[kind][0]), slot(g, to), send_line.at[g, ways.index((kind, distance))],
            slot_recv.at[g, to], in_line(kind, distance),
        )

    def forward(g, j):
        for kind, distance in ways:
            if kinds[kind][0] == j:
                when(there(kind, distance), lambda: line_copy(g, kind, distance).start())
        when(goes_next(j), lambda: next_copy(g, j).start())

    def relay(g, j):
        def work():
            remote(
                slot(g, j), slot(g, j), send_next.at[g, 0], slot_recv.at[g, j], sibling
            ).wait_recv()
            forward(g, j)

        when(exists(j), work)

    def each(work, begin=0, count=groups):
        def body(i, _):
            work(begin + i)
            return 0

        lax.fori_loop(0, count, body, 0)

    def out(slots, begin, count=1):
        for j in slots:
            each(lambda g: relay(g, j), begin, count)

    def own(g):
        wait_in(2, g)
        wait_in(3, g)
        forward(g, 0)

    def span(j):
        return pl.ds((SLOTS - j) * block, block)

    def add(g, j, source, sem):
        remote(source, source, grad_send.at[g, 0], sem, sibling).wait_recv()
        acc[g, :, span(j), :] += source[...].astype(jnp.float32)

    def give(g, j, place, sem, device):
        return remote(stage.at[g, j], place, grad_send.at[g, j], sem, device)

    def send_back(g, j, action):
        for index, (kind, distance) in enumerate(ways):
            if landing(kind, distance) == j:
                when(
                    back(kind, distance),
                    lambda: action(
                        give(
                            g, j, from_line.at[g, index], line_recv.at[g, index],
                            in_line_back(kind, distance),
                        )
                    ),
                )
        when(
            comes_earlier(j),
            lambda: action(
                give(g, j, from_next.at[g, j - LINE], next_recv.at[g, j - LINE], earlier)
            ),
        )

    def give_back(g, j, condition):
        def work():
            for index, (kind, distance) in enumerate(ways):
                if kinds[kind][0] == j:
                    when(
                        there(kind, distance),
                        lambda: add(g, j, from_line.at[g, index], line_recv.at[g, index]),
                    )
            when(goes_next(j), lambda: add(g, j, from_next.at[g, j], next_recv.at[g, j]))
            total = acc[g, :, span(j), :]
            if j == 0:
                stage[g, 0, 0] = (total[0] * SCALE).astype(jnp.bfloat16)
                stage[g, 0, 1] = total[1].astype(jnp.bfloat16)
                start_out(2, g)
                start_out(3, g)
            else:
                stage[g, j] = total.astype(jnp.bfloat16)
                send_back(g, j, lambda copy: copy.start())

        when(condition, work)

    chained = cross & (z > 0)

    def leaves(g):
        for j in range(LINE + 1, SLOTS):
            give_back(g, j, exists(j))
        give_back(g, SLOTS, exists(SLOTS) & jnp.logical_not(chained))

    def home(g, *slots):
        for j in slots:
            give_back(g, j, chained if j == SLOTS else exists(j))

    def gather_rows(g):
        wait_in(0, g)
        wait_in(1, g)
        for r in range(repeat):
            place = pl.ds(r * block, block)
            cols = pl.ds(r * HEAD_SIZE, HEAD_SIZE)
            qs[place, :] = qb[g, :, cols]
            cs[place, :] = cb[g, :, cols]

    def spread_rows(g):
        for r in range(repeat):
            place = pl.ds(r * block, block)
            cols = pl.ds(r * HEAD_SIZE, HEAD_SIZE)
            ob[g, :, cols] = os[place, :]
            gb[g, :, cols] = gs[place, :]
        start_out(0, g)
        start_out(1, g)

    def attend(g):
        gather_rows(g)
        key, value = kv[g, 0], kv[g, 1]
        key_t[...] = key.T
        value_t[...] = value.T
        tiles = [pl.ds(n * TILE, TILE) for n in range(stacked // TILE)]

        def score(place):
            raw = dot(key, qs[place, :], 1, 1) * (SCALE * math.log2(math.e))
            return raw + bias[:, place]

        scores = score(tiles[0])
        for n, place in enumerate(tiles):
            later_scores = score(tiles[n + 1]) if n + 1 < len(tiles) else None
            top = jnp.max(scores, 0, keepdims=True)
            e = jnp.exp2(scores - top)
            inverse = 1.0 / jnp.sum(e, 0, keepdims=True)
            e_half = e.astype(jnp.bfloat16)
            e_all[:, place] = e_half
            cot_t = (cs[place, :].astype(jnp.float32).T * inverse).astype(jnp.bfloat16)
            cot_n[place, :] = cot_t.astype(jnp.float32).T.astype(jnp.bfloat16)
            out_t = dot(value_t[...], e_half, 1, 0) * inverse
            out_half = out_t.astype(jnp.bfloat16).astype(jnp.float32)
            delta = jnp.sum(out_half * cot_t.astype(jnp.float32), 0, keepdims=True)
            score_grad = (e * (dot(value, cot_t, 1, 0) - delta)).astype(jnp.bfloat16)
            grad_all[:, place] = score_grad
            query_grad_t = dot(key_t[...], score_grad, 1, 0) * SCALE
            os[place, :] = out_half.T.astype(jnp.bfloat16)
            gs[place, :] = query_grad_t.T.astype(jnp.bfloat16)
            scores = later_scores
        acc[g, 1] = dot(e_all[...], cot_n[...], 1, 0)
        acc[g, 0] = dot(grad_all[...], qs[...], 1, 0)
        spread_rows(g)

    barrier = pltpu.get_barrier_semaphore()

    def greet(device):
        pl.semaphore_signal(barrier, inc=1, device_id=device, device_id_type=MESH)

    greet(sibling)
    friends = 1
    neighbours = [(has_next, later), (has_prev, earlier)]
    for distance in range(1, LINE):
        neighbours.append((z + distance < LINE, (s, h + 2 * distance)))
        neighbours.append((z >= distance, (s, h - 2 * distance)))
    for near, device in neighbours:
        when(near, lambda: greet(device))
        friends = friends + near.astype(jnp.int32)
    pl.semaphore_wait(barrier, friends)

    def open_keys(g):
        start_in(2, g)
        start_in(3, g)

    def open_rows(g):
        start_in(0, g)
        start_in(1, g)

    def blanks(g):
        for j in range(1, SLOTS + 1):

            def blank(j=j):
                kv[g, :, span(j), :] = jnp.zeros((2, block, HEAD_SIZE), jnp.bfloat16)

            pl.when(jnp.logical_not(exists(j)))(blank)

    each(open_keys)
    each(open_rows)
    each(own)
    each(blanks)
    place = lax.broadcasted_iota(jnp.int32, (window, stacked), 0)
    seen = (place >= bounds_ref[0:1, :]) & (place <= bounds_ref[1:2, :])
    bias[...] = jnp.where(seen, 0.0, HIDDEN)
    out([LINE], 0, groups)
    out([1, 2, 3], 0, 2)
    out([SLOTS], 0)

    def step(i, _):
        @pl.when(i < groups)
        def _():
            out([5, 6, 7], i)

        @pl.when(i + 1 < groups)
        def _():
            out([SLOTS], i + 1)

        @pl.when(i < groups)
        def _():
            attend(i)
            leaves(i)

        @pl.when(i + 2 < groups)
        def _():
            out([1, 2, 3], i + 2)

        @pl.when((i >= 1) & (i <= groups))
        def _():
            home(i - 1, 1, 2, 3, SLOTS)

        @pl.when(i >= 2)
        def _():
            home(i - 2, LINE, 0)

        return 0

    lax.fori_loop(0, groups + 2, step, 0)

    def close(g, _):
        for index in range(4):
            wait_out(index, g)
        for j in range(SLOTS + 1):
            when(goes_next(j), lambda: next_copy(g, j).wait_send())
            if j > 0:
                send_back(g, j, lambda copy: copy.wait_send())
        for kind, distance in ways:
            when(there(kind, distance), lambda: line_copy(g, kind, distance).wait_send())
        return 0

    lax.fori_loop(0, groups, close, 0)


def shard(queries, keys, values, output_cotangent, doc_ids):
    shards = lax.axis_size("seq")
    rows = queries.shape[0]
    block = 2 * rows
    window = (SLOTS + 1) * block
    groups = keys.shape[1] // HEAD_SIZE // 2
    repeat = queries.shape[1] // keys.shape[1]
    stacked = repeat * block
    wide = repeat * HEAD_SIZE

    origin = (lax.axis_index("seq") * LINE + lax.axis_index("head") // 2) * block
    base = jnp.maximum(origin - SLOTS * block, 0)
    near = lax.dynamic_slice(doc_ids, (base,), (window,))
    here = lax.dynamic_slice(doc_ids, (origin,), (block,))
    begin = base + jnp.sum((near[None, :] < here[:, None]).astype(jnp.int32), 1)
    begin = begin - (origin - SLOTS * block)
    end = SLOTS * block + jnp.arange(block, dtype=jnp.int32)
    bounds = jnp.stack([jnp.tile(begin, repeat), jnp.tile(end, repeat)])

    bf16, f32 = jnp.bfloat16, jnp.float32
    any_spec = pl.BlockSpec(memory_space=pl.ANY)
    dma = pltpu.SemaphoreType.DMA
    pair = (2, block, HEAD_SIZE)
    results = pl.pallas_call(
        functools.partial(kernel, shards, groups, repeat, rows),
        out_shape=(
            jax.ShapeDtypeStruct(queries.shape, bf16),
            jax.ShapeDtypeStruct(queries.shape, bf16),
            jax.ShapeDtypeStruct(keys.shape, bf16),
            jax.ShapeDtypeStruct(keys.shape, bf16),
        ),
        in_specs=[any_spec] * 4 + [pl.BlockSpec(memory_space=pltpu.VMEM)],
        out_specs=[any_spec] * 4,
        scratch_shapes=[
            pltpu.VMEM((groups, block, wide), bf16),
            pltpu.VMEM((groups, block, wide), bf16),
            pltpu.VMEM((groups, block, wide), bf16),
            pltpu.VMEM((groups, block, wide), bf16),
            pltpu.VMEM((groups, 2, window, HEAD_SIZE), bf16),
            pltpu.VMEM((window, stacked), f32),
            pltpu.VMEM((groups, 2, window, HEAD_SIZE), f32),
            pltpu.VMEM((stacked, HEAD_SIZE), bf16),
            pltpu.VMEM((stacked, HEAD_SIZE), bf16),
            pltpu.VMEM((stacked, HEAD_SIZE), bf16),
            pltpu.VMEM((stacked, HEAD_SIZE), bf16),
            pltpu.VMEM((groups, SLOTS + 1) + pair, bf16),
            pltpu.VMEM((groups, LINE + 1) + pair, bf16),
            pltpu.VMEM((groups, 4 * (LINE - 1)) + pair, bf16),
            pltpu.VMEM((HEAD_SIZE, window), bf16),
            pltpu.VMEM((HEAD_SIZE, window), bf16),
            pltpu.VMEM((window, stacked), bf16),
            pltpu.VMEM((window, stacked), bf16),
            pltpu.VMEM((stacked, HEAD_SIZE), bf16),
            dma((groups, 4)), dma((groups, 4)), dma((groups, 4)),
            dma((groups, 4)), dma((groups, 4)), dma((groups, 4)),
            dma((groups, LINE + 1)), dma((groups, 4 * (LINE - 1))), dma((groups, SLOTS + 1)),
            dma((groups, SLOTS + 1)), dma((groups, LINE + 1)), dma((groups, 4 * (LINE - 1))),
        ],
        compiler_params=pltpu.CompilerParams(
            collective_id=0, has_side_effects=True, vmem_limit_bytes=56 * 1024 * 1024
        ),
    )(queries, keys, values, output_cotangent, bounds)
    steps = 4
    blocks = [pl.BlockSpec((rows, r.shape[1] // steps), lambda i: (0, i)) for r in results]
    return pl.pallas_call(
        hand_on,
        out_shape=tuple(jax.ShapeDtypeStruct(r.shape, r.dtype) for r in results),
        grid=(steps,),
        in_specs=blocks,
        out_specs=blocks,
    )(*results)


def solution(mesh):
    tokens = P(("seq", "head"), None)
    return jax.shard_map(
        shard,
        mesh=mesh,
        in_specs=(tokens, tokens, tokens, tokens, P()),
        out_specs=(tokens, tokens, tokens, tokens),
        check_vma=False,
    )
```

```python
import functools
import math

import jax
import jax.numpy as jnp
from jax import lax
from jax.experimental import pallas as pl
from jax.experimental.pallas import tpu as pltpu
from jax.sharding import PartitionSpec as P

MESH = pl.DeviceIdType.MESH
HEAD_SIZE = 128
SLOTS = 8
LINE = 4
SCALE = HEAD_SIZE**-0.5
TILE = 256
HIDDEN = -1e30


def dot(left, right, left_dim, right_dim):
    return lax.dot_general(
        left, right, (((left_dim,), (right_dim,)), ((), ())), preferred_element_type=jnp.float32
    )


def hand_on(*refs):
    for i in range(4):
        refs[4 + i][...] = refs[i][...]


def kernel(
    shards, groups, repeat, rows,
    q_ref, k_ref, v_ref, c_ref, bounds_ref,
    out_ref, dq_ref, dk_ref, dv_ref,
    qb, cb, ob, gb, kv, bias, acc, qs, cs, os, gs, stage, from_next, from_line,
    key_t, value_t, e_all, grad_all, cot_n, raw, prob_grad,
    x_send, x_recv, x_local, o_send, o_recv, o_local,
    send_next, send_line, slot_recv, grad_send, next_recv, line_recv,
):
    block = 2 * rows
    window = (SLOTS + 1) * block
    stacked = repeat * block
    wide = repeat * HEAD_SIZE
    s, h = lax.axis_index("seq"), lax.axis_index("head")
    z, k = lax.div(h, 2), lax.rem(h, 2)
    sibling = (s, h + 1 - 2 * k)
    first, cross, gate = s == 0, s == shards // 2, s == shards // 2 - 1
    has_next, has_prev = s < shards - 1, s > 0
    later, earlier = (s + 1, h), (s - 1, h)

    def exists(j):
        return s * LINE + z >= j

    def goes_next(j):
        if j > LINE:
            return None
        there = has_next & exists(j)
        return there if j % LINE == 0 else there & jnp.logical_not(gate)

    def comes_earlier(j):
        if j < LINE:
            return None
        return exists(j) if j % LINE == 0 else exists(j) & jnp.logical_not(cross)

    kinds = ((0, 1), (LINE, -1), (LINE, 1), (SLOTS, -1))
    allowed = (s >= 0, jnp.logical_not(first), cross, cross)

    def there(kind, distance):
        place = z + kinds[kind][1] * distance
        return allowed[kind] & (place >= 0) & (place < LINE)

    def back(kind, distance):
        place = z - kinds[kind][1] * distance
        return allowed[kind] & (place >= 0) & (place < LINE)

    def in_line(kind, distance):
        return (s, h + 2 * kinds[kind][1] * distance)

    def in_line_back(kind, distance):
        return (s, h - 2 * kinds[kind][1] * distance)

    def landing(kind, distance):
        return kinds[kind][0] + kinds[kind][1] * distance

    ways = [(kind, distance) for kind in range(4) for distance in range(1, LINE)]

    def slot(g, j):
        return kv.at[g, :, pl.ds((SLOTS - j) * block, block), :]

    def remote(src, dst, send, recv, device):
        return pltpu.make_async_remote_copy(
            src_ref=src, dst_ref=dst, send_sem=send, recv_sem=recv,
            device_id=device, device_id_type=MESH,
        )

    def when(condition, work):
        if condition is not None:
            pl.when(condition)(work)

    def columns(core, g, width):
        start = (core * groups + g) * width
        return pl.ds(pl.multiple_of(start, HEAD_SIZE), width)

    mine = pl.ds(pl.multiple_of(k * rows, 16), rows)
    theirs = pl.ds(pl.multiple_of((1 - k) * rows, 16), rows)
    mine_tail = pl.ds(pl.multiple_of(SLOTS * block + k * rows, 16), rows)

    def in_place(index, g):
        return (
            lambda: qb.at[g, mine, :], lambda: cb.at[g, mine, :],
            lambda: kv.at[g, 0, mine_tail, :], lambda: kv.at[g, 1, mine_tail, :],
        )[index]()

    def in_copies(index, g):
        source = (q_ref, c_ref, k_ref, v_ref)[index]
        width = wide if index < 2 else HEAD_SIZE
        local = pltpu.make_async_copy(
            source.at[:, columns(k, g, width)], in_place(index, g), x_local.at[g, index]
        )
        over = remote(
            source.at[:, columns(1 - k, g, width)], in_place(index, g),
            x_send.at[g, index], x_recv.at[g, index], sibling,
        )
        return local, over

    def start_in(index, g):
        local, over = in_copies(index, g)
        over.start()
        local.start()

    def wait_in(index, g):
        local, over = in_copies(index, g)
        local.wait()
        over.wait()

    def out_copies(index, g):
        target = (out_ref, dq_ref, dk_ref, dv_ref)[index]
        width = wide if index < 2 else HEAD_SIZE

        def part(which):
            if index < 2:
                return (ob, gb)[index].at[g, which, :]
            return stage.at[g, 0, index - 2, which, :]

        place = target.at[:, columns(k, g, width)]
        local = pltpu.make_async_copy(part(mine), place, o_local.at[g, index])
        over = remote(part(theirs), place, o_send.at[g, index], o_recv.at[g, index], sibling)
        return local, over

    def start_out(index, g):
        local, over = out_copies(index, g)
        over.start()
        local.start()

    def wait_out(index, g):
        local, over = out_copies(index, g)
        local.wait()
        over.wait()

    def next_copy(g, j):
        return remote(
            slot(g, j), slot(g, j + LINE), send_next.at[g, j], slot_recv.at[g, j + LINE], later
        )

    def line_copy(g, kind, distance):
        to = landing(kind, distance)
        return remote(
            slot(g, kinds[kind][0]), slot(g, to), send_line.at[g, ways.index((kind, distance))],
            slot_recv.at[g, to], in_line(kind, distance),
        )

    def forward(g, j):
        for kind, distance in ways:
            if kinds[kind][0] == j:
                when(there(kind, distance), lambda: line_copy(g, kind, distance).start())
        when(goes_next(j), lambda: next_copy(g, j).start())

    def relay(g, j):
        def work():
            remote(
                slot(g, j), slot(g, j), send_next.at[g, 0], slot_recv.at[g, j], sibling
            ).wait_recv()
            forward(g, j)

        when(exists(j), work)

    def each(work, begin=0, count=groups):
        def body(i, _):
            work(begin + i)
            return 0

        lax.fori_loop(0, count, body, 0)

    def out(slots, begin, count=1):
        for j in slots:
            each(lambda g: relay(g, j), begin, count)

    def own(g):
        wait_in(2, g)
        wait_in(3, g)
        forward(g, 0)

    def span(j):
        return pl.ds((SLOTS - j) * block, block)

    def add(g, j, source, sem):
        remote(source, source, grad_send.at[g, 0], sem, sibling).wait_recv()
        acc[g, :, span(j), :] += source[...].astype(jnp.float32)

    def give(g, j, place, sem, device):
        return remote(stage.at[g, j], place, grad_send.at[g, j], sem, device)

    def send_back(g, j, action):
        for index, (kind, distance) in enumerate(ways):
            if landing(kind, distance) == j:
                when(
                    back(kind, distance),
                    lambda: action(
                        give(
                            g, j, from_line.at[g, index], line_recv.at[g, index],
                            in_line_back(kind, distance),
                        )
                    ),
                )
        when(
            comes_earlier(j),
            lambda: action(
                give(g, j, from_next.at[g, j - LINE], next_recv.at[g, j - LINE], earlier)
            ),
        )

    def give_back(g, j, condition):
        def work():
            for index, (kind, distance) in enumerate(ways):
                if kinds[kind][0] == j:
                    when(
                        there(kind, distance),
                        lambda: add(g, j, from_line.at[g, index], line_recv.at[g, index]),
                    )
            when(goes_next(j), lambda: add(g, j, from_next.at[g, j], next_recv.at[g, j]))
            total = acc[g, :, span(j), :]
            if j == 0:
                stage[g, 0, 0] = (total[0] * SCALE).astype(jnp.bfloat16)
                stage[g, 0, 1] = total[1].astype(jnp.bfloat16)
                start_out(2, g)
                start_out(3, g)
            else:
                stage[g, j] = total.astype(jnp.bfloat16)
                send_back(g, j, lambda copy: copy.start())

        when(condition, work)

    chained = cross & (z > 0)

    def leaves(g):
        for j in range(LINE + 1, SLOTS):
            give_back(g, j, exists(j))
        give_back(g, SLOTS, exists(SLOTS) & jnp.logical_not(chained))

    def home(g, *slots):
        for j in slots:
            give_back(g, j, chained if j == SLOTS else exists(j))

    def gather_rows(g):
        wait_in(0, g)
        wait_in(1, g)
        for r in range(repeat):
            place = pl.ds(r * block, block)
            cols = pl.ds(r * HEAD_SIZE, HEAD_SIZE)
            qs[place, :] = qb[g, :, cols]
            cs[place, :] = cb[g, :, cols]

    def spread_rows(g):
        for r in range(repeat):
            place = pl.ds(r * block, block)
            cols = pl.ds(r * HEAD_SIZE, HEAD_SIZE)
            ob[g, :, cols] = os[place, :]
            gb[g, :, cols] = gs[place, :]
        start_out(0, g)
        start_out(1, g)

    def attend(g):
        gather_rows(g)
        key, value = kv[g, 0], kv[g, 1]
        key_t[...] = key.T
        value_t[...] = value.T
        tiles = [pl.ds(n * TILE, TILE) for n in range(stacked // TILE)]
        pieces = [pl.ds(i * block, block) for i in range(SLOTS + 1)]
        exponent = SCALE * math.log2(math.e)

        raw[0] = dot(key, qs[tiles[0], :], 1, 1)
        for n, place in enumerate(tiles):
            if n + 1 < len(tiles):
                raw[(n + 1) % 2] = dot(key, qs[tiles[n + 1], :], 1, 1)
            now = raw.at[n % 2]
            top = jnp.full((1, TILE), HIDDEN, jnp.float32)
            for piece in pieces:
                top = jnp.maximum(top, jnp.max(now[piece, :] + bias[piece, place], 0, keepdims=True))
            top = top * exponent
            total = jnp.zeros((1, TILE), jnp.float32)
            for piece in pieces:
                e = jnp.exp2(now[piece, :] * exponent - top + bias[piece, place])
                total = total + jnp.sum(e, 0, keepdims=True)
                e_all[piece, place] = e.astype(jnp.bfloat16)
            inverse = 1.0 / total
            cot_t = (cs[place, :].astype(jnp.float32).T * inverse).astype(jnp.bfloat16)
            cot_n[place, :] = cot_t.astype(jnp.float32).T.astype(jnp.bfloat16)
            prob_grad[...] = dot(value, cot_t, 1, 0)
            out_t = dot(value_t[...], e_all[:, place], 1, 0) * inverse
            out_half = out_t.astype(jnp.bfloat16).astype(jnp.float32)
            delta = jnp.sum(out_half * cot_t.astype(jnp.float32), 0, keepdims=True)
            for piece in pieces:
                e = e_all[piece, place].astype(jnp.float32)
                grad_all[piece, place] = (e * (prob_grad[piece, :] - delta)).astype(jnp.bfloat16)
            query_grad_t = dot(key_t[...], grad_all[:, place], 1, 0) * SCALE
            os[place, :] = out_half.T.astype(jnp.bfloat16)
            gs[place, :] = query_grad_t.T.astype(jnp.bfloat16)
        acc[g, 1] = dot(e_all[...], cot_n[...], 1, 0)
        acc[g, 0] = dot(grad_all[...], qs[...], 1, 0)
        spread_rows(g)

    barrier = pltpu.get_barrier_semaphore()

    def greet(device):
        pl.semaphore_signal(barrier, inc=1, device_id=device, device_id_type=MESH)

    greet(sibling)
    friends = 1
    neighbours = [(has_next, later), (has_prev, earlier)]
    for distance in range(1, LINE):
        neighbours.append((z + distance < LINE, (s, h + 2 * distance)))
        neighbours.append((z >= distance, (s, h - 2 * distance)))
    for near, device in neighbours:
        when(near, lambda: greet(device))
        friends = friends + near.astype(jnp.int32)
    pl.semaphore_wait(barrier, friends)

    def open_keys(g):
        start_in(2, g)
        start_in(3, g)

    def open_rows(g):
        start_in(0, g)
        start_in(1, g)

    def blanks(g):
        for j in range(1, SLOTS + 1):

            def blank(j=j):
                kv[g, :, span(j), :] = jnp.zeros((2, block, HEAD_SIZE), jnp.bfloat16)

            pl.when(jnp.logical_not(exists(j)))(blank)

    each(open_keys)
    each(open_rows)
    own(0)
    each(blanks)
    place = lax.broadcasted_iota(jnp.int32, (window, stacked), 0)
    seen = (place >= bounds_ref[0:1, :]) & (place <= bounds_ref[1:2, :])
    bias[...] = jnp.where(seen, 0.0, HIDDEN)

    def begin(g):
        pl.when(g + 1 < groups)(lambda: own(g + 1))
        relay(g, LINE)

    each(begin)
    out([1, 2, 3], 0, 2)
    out([SLOTS], 0)

    def step(i, _):
        @pl.when(i < groups)
        def _():
            out([5, 6, 7], i)

        @pl.when(i + 1 < groups)
        def _():
            out([SLOTS], i + 1)

        @pl.when(i < groups)
        def _():
            attend(i)
            leaves(i)

        @pl.when(i + 2 < groups)
        def _():
            out([1, 2, 3], i + 2)

        @pl.when((i >= 1) & (i <= groups))
        def _():
            home(i - 1, 1, 2, 3, SLOTS)

        @pl.when(i >= 2)
        def _():
            home(i - 2, LINE, 0)

        return 0

    lax.fori_loop(0, groups + 2, step, 0)

    def close(g, _):
        for index in range(4):
            wait_out(index, g)
        for j in range(SLOTS + 1):
            when(goes_next(j), lambda: next_copy(g, j).wait_send())
            if j > 0:
                send_back(g, j, lambda copy: copy.wait_send())
        for kind, distance in ways:
            when(there(kind, distance), lambda: line_copy(g, kind, distance).wait_send())
        return 0

    lax.fori_loop(0, groups, close, 0)


def shard(queries, keys, values, output_cotangent, doc_ids):
    shards = lax.axis_size("seq")
    rows = queries.shape[0]
    block = 2 * rows
    window = (SLOTS + 1) * block
    groups = keys.shape[1] // HEAD_SIZE // 2
    repeat = queries.shape[1] // keys.shape[1]
    stacked = repeat * block
    wide = repeat * HEAD_SIZE

    origin = (lax.axis_index("seq") * LINE + lax.axis_index("head") // 2) * block
    base = jnp.maximum(origin - SLOTS * block, 0)
    near = lax.dynamic_slice(doc_ids, (base,), (window,))
    here = lax.dynamic_slice(doc_ids, (origin,), (block,))
    begin = base + jnp.sum((near[None, :] < here[:, None]).astype(jnp.int32), 1)
    begin = begin - (origin - SLOTS * block)
    end = SLOTS * block + jnp.arange(block, dtype=jnp.int32)
    bounds = jnp.stack([jnp.tile(begin, repeat), jnp.tile(end, repeat)])

    bf16, f32 = jnp.bfloat16, jnp.float32
    any_spec = pl.BlockSpec(memory_space=pl.ANY)
    dma = pltpu.SemaphoreType.DMA
    pair = (2, block, HEAD_SIZE)
    results = pl.pallas_call(
        functools.partial(kernel, shards, groups, repeat, rows),
        out_shape=(
            jax.ShapeDtypeStruct(queries.shape, bf16),
            jax.ShapeDtypeStruct(queries.shape, bf16),
            jax.ShapeDtypeStruct(keys.shape, bf16),
            jax.ShapeDtypeStruct(keys.shape, bf16),
        ),
        in_specs=[any_spec] * 4 + [pl.BlockSpec(memory_space=pltpu.VMEM)],
        out_specs=[any_spec] * 4,
        scratch_shapes=[
            pltpu.VMEM((groups, block, wide), bf16),
            pltpu.VMEM((groups, block, wide), bf16),
            pltpu.VMEM((groups, block, wide), bf16),
            pltpu.VMEM((groups, block, wide), bf16),
            pltpu.VMEM((groups, 2, window, HEAD_SIZE), bf16),
            pltpu.VMEM((window, stacked), f32),
            pltpu.VMEM((groups, 2, window, HEAD_SIZE), f32),
            pltpu.VMEM((stacked, HEAD_SIZE), bf16),
            pltpu.VMEM((stacked, HEAD_SIZE), bf16),
            pltpu.VMEM((stacked, HEAD_SIZE), bf16),
            pltpu.VMEM((stacked, HEAD_SIZE), bf16),
            pltpu.VMEM((groups, SLOTS + 1) + pair, bf16),
            pltpu.VMEM((groups, LINE + 1) + pair, bf16),
            pltpu.VMEM((groups, 4 * (LINE - 1)) + pair, bf16),
            pltpu.VMEM((HEAD_SIZE, window), bf16),
            pltpu.VMEM((HEAD_SIZE, window), bf16),
            pltpu.VMEM((window, stacked), bf16),
            pltpu.VMEM((window, stacked), bf16),
            pltpu.VMEM((stacked, HEAD_SIZE), bf16),
            pltpu.VMEM((2, window, TILE), f32),
            pltpu.VMEM((window, TILE), f32),
            dma((groups, 4)), dma((groups, 4)), dma((groups, 4)),
            dma((groups, 4)), dma((groups, 4)), dma((groups, 4)),
            dma((groups, LINE + 1)), dma((groups, 4 * (LINE - 1))), dma((groups, SLOTS + 1)),
            dma((groups, SLOTS + 1)), dma((groups, LINE + 1)), dma((groups, 4 * (LINE - 1))),
        ],
        compiler_params=pltpu.CompilerParams(
            collective_id=0, has_side_effects=True, vmem_limit_bytes=56 * 1024 * 1024
        ),
    )(queries, keys, values, output_cotangent, bounds)
    steps = 4
    blocks = [pl.BlockSpec((rows, r.shape[1] // steps), lambda i: (0, i)) for r in results]
    return pl.pallas_call(
        hand_on,
        out_shape=tuple(jax.ShapeDtypeStruct(r.shape, r.dtype) for r in results),
        grid=(steps,),
        in_specs=blocks,
        out_specs=blocks,
    )(*results)


def solution(mesh):
    tokens = P(("seq", "head"), None)
    return jax.shard_map(
        shard,
        mesh=mesh,
        in_specs=(tokens, tokens, tokens, tokens, P()),
        out_specs=(tokens, tokens, tokens, tokens),
        check_vma=False,
    )
```

```python
import functools
import math

import jax
import jax.numpy as jnp
from jax import lax
from jax.experimental import pallas as pl
from jax.experimental.pallas import tpu as pltpu
from jax.sharding import PartitionSpec as P

MESH = pl.DeviceIdType.MESH
HEAD_SIZE = 128
SLOTS = 8
LINE = 4
SCALE = HEAD_SIZE**-0.5
TILE = 256
HIDDEN = -1e30
WAYS = 16


def dot(left, right, left_dim, right_dim):
    return lax.dot_general(
        left, right, (((left_dim,), (right_dim,)), ((), ())), preferred_element_type=jnp.float32
    )


def hand_on(*refs):
    for i in range(4):
        refs[4 + i][...] = refs[i][...]


def kernel(
    shards, groups, repeat, rows,
    q_ref, k_ref, v_ref, c_ref, bounds_ref,
    out_ref, dq_ref, dk_ref, dv_ref,
    qb, cb, ob, gb, kv, bias, acc, qs, cs, os, gs, stage, from_next, from_line,
    key_t, value_t, e_all, grad_all, cot_n, raw, prob_grad,
    x_send, x_recv, x_local, o_send, o_recv, o_local,
    send_next, send_line, slot_recv, grad_send, next_recv, line_recv,
):
    block = 2 * rows
    window = (SLOTS + 1) * block
    stacked = repeat * block
    wide = repeat * HEAD_SIZE
    s, h = lax.axis_index("seq"), lax.axis_index("head")
    z, k = lax.div(h, 2), lax.rem(h, 2)
    sibling = (s, h + 1 - 2 * k)
    first, cross, gate = s == 0, s == shards // 2, s == shards // 2 - 1
    has_next, has_prev = s < shards - 1, s > 0
    later, earlier = (s + 1, h), (s - 1, h)

    def exists(j):
        return s * LINE + z >= j

    def goes_next(j):
        if j > LINE:
            return None
        there = has_next & exists(j)
        return there if j % LINE == 0 else there & jnp.logical_not(gate)

    def comes_earlier(j):
        if j < LINE:
            return None
        return exists(j) if j % LINE == 0 else exists(j) & jnp.logical_not(cross)

    near = range(1, LINE)
    ways = [(0, d) for d in near] + [(LINE, -d) for d in near] + [(SLOTS, -d) for d in near]
    ways += [(1, 1), (2, 1), (4, 1), (5, 1), (6, 1), (2, -1), (3, -1)]

    def rule(way, place):
        j, move = way
        inside = (place + move >= 0) & (place + move < LINE)
        if (j == 0 and move > 0) or (j == LINE and move < 0):
            straight = inside if abs(move) == 1 else inside & jnp.logical_not(cross)
            return straight if j == 0 else straight & jnp.logical_not(first)
        if j == SLOTS:
            return inside & cross
        return inside & cross & ((place >= j % LINE) if move > 0 else (place < j))

    def there(way):
        return rule(way, z)

    def back(way):
        place = z - way[1]
        return rule(way, place) & (place >= 0) & (place < LINE)

    def climbs(j):
        return cross & (z >= j - LINE)

    def busy(j):
        return functools.reduce(lambda a, b: a | b, [there(w) for w in ways if w[0] == j])

    def slot(g, j):
        return kv.at[g, :, pl.ds((SLOTS - j) * block, block), :]

    def remote(src, dst, send, recv, device):
        return pltpu.make_async_remote_copy(
            src_ref=src, dst_ref=dst, send_sem=send, recv_sem=recv,
            device_id=device, device_id_type=MESH,
        )

    def when(condition, work):
        if condition is not None:
            pl.when(condition)(work)

    def columns(core, g, width):
        start = (core * groups + g) * width
        return pl.ds(pl.multiple_of(start, HEAD_SIZE), width)

    mine = pl.ds(pl.multiple_of(k * rows, 16), rows)
    theirs = pl.ds(pl.multiple_of((1 - k) * rows, 16), rows)
    mine_tail = pl.ds(pl.multiple_of(SLOTS * block + k * rows, 16), rows)

    def in_place(index, g):
        return (
            lambda: qb.at[g, mine, :], lambda: cb.at[g, mine, :],
            lambda: kv.at[g, 0, mine_tail, :], lambda: kv.at[g, 1, mine_tail, :],
        )[index]()

    def in_copies(index, g):
        source = (q_ref, c_ref, k_ref, v_ref)[index]
        width = wide if index < 2 else HEAD_SIZE
        local = pltpu.make_async_copy(
            source.at[:, columns(k, g, width)], in_place(index, g), x_local.at[g, index]
        )
        over = remote(
            source.at[:, columns(1 - k, g, width)], in_place(index, g),
            x_send.at[g, index], x_recv.at[g, index], sibling,
        )
        return local, over

    def start_in(index, g):
        local, over = in_copies(index, g)
        over.start()
        local.start()

    def wait_in(index, g):
        local, over = in_copies(index, g)
        local.wait()
        over.wait()

    def out_copies(index, g):
        target = (out_ref, dq_ref, dk_ref, dv_ref)[index]
        width = wide if index < 2 else HEAD_SIZE

        def part(which):
            if index < 2:
                return (ob, gb)[index].at[g, which, :]
            return stage.at[g, 0, index - 2, which, :]

        place = target.at[:, columns(k, g, width)]
        local = pltpu.make_async_copy(part(mine), place, o_local.at[g, index])
        over = remote(part(theirs), place, o_send.at[g, index], o_recv.at[g, index], sibling)
        return local, over

    def start_out(index, g):
        local, over = out_copies(index, g)
        over.start()
        local.start()

    def wait_out(index, g):
        local, over = out_copies(index, g)
        local.wait()
        over.wait()

    def next_copy(g, j):
        return remote(
            slot(g, j), slot(g, j + LINE), send_next.at[g, j], slot_recv.at[g, j + LINE], later
        )

    def line_copy(g, way):
        j, move = way
        return remote(
            slot(g, j), slot(g, j + move), send_line.at[g, ways.index(way)],
            slot_recv.at[g, j + move], (s, h + 2 * move),
        )

    def forward(g, j):
        for way in ways:
            if way[0] == j:
                when(there(way), lambda: line_copy(g, way).start())
        when(goes_next(j), lambda: next_copy(g, j).start())

    def relay(g, j, condition):
        def work():
            remote(
                slot(g, j), slot(g, j), send_next.at[g, 0], slot_recv.at[g, j], sibling
            ).wait_recv()
            forward(g, j)

        when(condition, work)

    def each(work, begin=0, count=groups):
        def body(i, _):
            work(begin + i)
            return 0

        lax.fori_loop(0, count, body, 0)

    def early(g):
        for j in range(1, LINE):
            relay(g, j, exists(j))
        for j in range(LINE + 1, SLOTS):
            relay(g, j, climbs(j))

    def late(g):
        relay(g, SLOTS, exists(SLOTS))
        for j in range(LINE + 1, SLOTS):
            relay(g, j, exists(j) & jnp.logical_not(climbs(j)))

    def own(g):
        wait_in(2, g)
        wait_in(3, g)
        forward(g, 0)

    def span(j):
        return pl.ds((SLOTS - j) * block, block)

    def add(g, j, source, sem):
        remote(source, source, grad_send.at[g, 0], sem, sibling).wait_recv()
        acc[g, :, span(j), :] += source[...].astype(jnp.float32)

    def give(g, j, place, sem, device):
        return remote(stage.at[g, j], place, grad_send.at[g, j], sem, device)

    def send_back(g, j, action):
        for index, way in enumerate(ways):
            if way[0] + way[1] == j:
                when(
                    back(way),
                    lambda: action(
                        give(
                            g, j, from_line.at[g, index], line_recv.at[g, index],
                            (s, h - 2 * way[1]),
                        )
                    ),
                )
        when(
            comes_earlier(j),
            lambda: action(
                give(g, j, from_next.at[g, j - LINE], next_recv.at[g, j - LINE], earlier)
            ),
        )

    def give_back(g, j, condition):
        def work():
            for index, way in enumerate(ways):
                if way[0] == j:
                    when(
                        there(way),
                        lambda: add(g, j, from_line.at[g, index], line_recv.at[g, index]),
                    )
            when(goes_next(j), lambda: add(g, j, from_next.at[g, j], next_recv.at[g, j]))
            total = acc[g, :, span(j), :]
            if j == 0:
                stage[g, 0, 0] = (total[0] * SCALE).astype(jnp.bfloat16)
                stage[g, 0, 1] = total[1].astype(jnp.bfloat16)
                start_out(2, g)
                start_out(3, g)
            else:
                stage[g, j] = total.astype(jnp.bfloat16)
                send_back(g, j, lambda copy: copy.start())

        when(condition, work)

    def leaves(g):
        for j in range(LINE + 1, SLOTS + 1):
            free = exists(j) if j == SLOTS - 1 else exists(j) & jnp.logical_not(busy(j))
            give_back(g, j, free)

    def middle(g):
        for j in (SLOTS, SLOTS - 2, SLOTS - 3):
            give_back(g, j, busy(j))
        for j in range(1, LINE):
            give_back(g, j, exists(j) & (z < j))
        for j in range(LINE - 1, 0, -1):
            give_back(g, j, z >= j)

    def last(g):
        give_back(g, LINE, exists(LINE))
        give_back(g, 0, s >= 0)

    def gather_rows(g):
        wait_in(0, g)
        wait_in(1, g)
        for r in range(repeat):
            place = pl.ds(r * block, block)
            cols = pl.ds(r * HEAD_SIZE, HEAD_SIZE)
            qs[place, :] = qb[g, :, cols]
            cs[place, :] = cb[g, :, cols]

    def spread_rows(g):
        for r in range(repeat):
            place = pl.ds(r * block, block)
            cols = pl.ds(r * HEAD_SIZE, HEAD_SIZE)
            ob[g, :, cols] = os[place, :]
            gb[g, :, cols] = gs[place, :]
        start_out(0, g)
        start_out(1, g)

    def attend(g):
        gather_rows(g)
        key, value = kv[g, 0], kv[g, 1]
        key_t[...] = key.T
        value_t[...] = value.T
        tiles = [pl.ds(n * TILE, TILE) for n in range(stacked // TILE)]
        pieces = [pl.ds(i * block, block) for i in range(SLOTS + 1)]
        exponent = SCALE * math.log2(math.e)

        raw[0] = dot(key, qs[tiles[0], :], 1, 1)
        for n, place in enumerate(tiles):
            if n + 1 < len(tiles):
                raw[(n + 1) % 2] = dot(key, qs[tiles[n + 1], :], 1, 1)
            now = raw.at[n % 2]
            top = jnp.full((1, TILE), HIDDEN, jnp.float32)
            for piece in pieces:
                top = jnp.maximum(top, jnp.max(now[piece, :] + bias[piece, place], 0, keepdims=True))
            top = top * exponent
            total = jnp.zeros((1, TILE), jnp.float32)
            for piece in pieces:
                e = jnp.exp2(now[piece, :] * exponent - top + bias[piece, place])
                total = total + jnp.sum(e, 0, keepdims=True)
                e_all[piece, place] = e.astype(jnp.bfloat16)
            inverse = 1.0 / total
            cot_t = (cs[place, :].astype(jnp.float32).T * inverse).astype(jnp.bfloat16)
            cot_n[place, :] = cot_t.astype(jnp.float32).T.astype(jnp.bfloat16)
            prob_grad[...] = dot(value, cot_t, 1, 0)
            out_t = dot(value_t[...], e_all[:, place], 1, 0) * inverse
            out_half = out_t.astype(jnp.bfloat16).astype(jnp.float32)
            delta = jnp.sum(out_half * cot_t.astype(jnp.float32), 0, keepdims=True)
            for piece in pieces:
                e = e_all[piece, place].astype(jnp.float32)
                grad_all[piece, place] = (e * (prob_grad[piece, :] - delta)).astype(jnp.bfloat16)
            query_grad_t = dot(key_t[...], grad_all[:, place], 1, 0) * SCALE
            os[place, :] = out_half.T.astype(jnp.bfloat16)
            gs[place, :] = query_grad_t.T.astype(jnp.bfloat16)
        acc[g, 1] = dot(e_all[...], cot_n[...], 1, 0)
        acc[g, 0] = dot(grad_all[...], qs[...], 1, 0)
        spread_rows(g)

    barrier = pltpu.get_barrier_semaphore()

    def greet(device):
        pl.semaphore_signal(barrier, inc=1, device_id=device, device_id_type=MESH)

    greet(sibling)
    friends = 1
    neighbours = [(has_next, later), (has_prev, earlier)]
    for distance in range(1, LINE):
        neighbours.append((z + distance < LINE, (s, h + 2 * distance)))
        neighbours.append((z >= distance, (s, h - 2 * distance)))
    for near, device in neighbours:
        when(near, lambda: greet(device))
        friends = friends + near.astype(jnp.int32)
    pl.semaphore_wait(barrier, friends)

    def open_keys(g):
        start_in(2, g)
        start_in(3, g)

    def open_rows(g):
        start_in(0, g)
        start_in(1, g)

    def blanks(g):
        for j in range(1, SLOTS + 1):

            def blank(j=j):
                kv[g, :, span(j), :] = jnp.zeros((2, block, HEAD_SIZE), jnp.bfloat16)

            pl.when(jnp.logical_not(exists(j)))(blank)

    each(open_keys)
    each(open_rows)
    own(0)
    each(blanks)
    place = lax.broadcasted_iota(jnp.int32, (window, stacked), 0)
    seen = (place >= bounds_ref[0:1, :]) & (place <= bounds_ref[1:2, :])
    bias[...] = jnp.where(seen, 0.0, HIDDEN)

    def begin(g):
        pl.when(g + 1 < groups)(lambda: own(g + 1))
        relay(g, LINE, exists(LINE))

    each(begin)
    each(early, 0, 2)

    def step(i, _):
        @pl.when(i < groups)
        def _():
            late(i)
            attend(i)
            leaves(i)

        @pl.when(i + 2 < groups)
        def _():
            early(i + 2)

        @pl.when((i >= 1) & (i <= groups))
        def _():
            middle(i - 1)

        @pl.when(i >= 2)
        def _():
            last(i - 2)

        return 0

    lax.fori_loop(0, groups + 2, step, 0)

    def close(g, _):
        for index in range(4):
            wait_out(index, g)
        for j in range(SLOTS + 1):
            when(goes_next(j), lambda: next_copy(g, j).wait_send())
            if j > 0:
                send_back(g, j, lambda copy: copy.wait_send())
        for way in ways:
            when(there(way), lambda: line_copy(g, way).wait_send())
        return 0

    lax.fori_loop(0, groups, close, 0)


def shard(queries, keys, values, output_cotangent, doc_ids):
    shards = lax.axis_size("seq")
    rows = queries.shape[0]
    block = 2 * rows
    window = (SLOTS + 1) * block
    groups = keys.shape[1] // HEAD_SIZE // 2
    repeat = queries.shape[1] // keys.shape[1]
    stacked = repeat * block
    wide = repeat * HEAD_SIZE

    origin = (lax.axis_index("seq") * LINE + lax.axis_index("head") // 2) * block
    base = jnp.maximum(origin - SLOTS * block, 0)
    near = lax.dynamic_slice(doc_ids, (base,), (window,))
    here = lax.dynamic_slice(doc_ids, (origin,), (block,))
    begin = base + jnp.sum((near[None, :] < here[:, None]).astype(jnp.int32), 1)
    begin = begin - (origin - SLOTS * block)
    end = SLOTS * block + jnp.arange(block, dtype=jnp.int32)
    bounds = jnp.stack([jnp.tile(begin, repeat), jnp.tile(end, repeat)])

    bf16, f32 = jnp.bfloat16, jnp.float32
    any_spec = pl.BlockSpec(memory_space=pl.ANY)
    dma = pltpu.SemaphoreType.DMA
    pair = (2, block, HEAD_SIZE)
    results = pl.pallas_call(
        functools.partial(kernel, shards, groups, repeat, rows),
        out_shape=(
            jax.ShapeDtypeStruct(queries.shape, bf16),
            jax.ShapeDtypeStruct(queries.shape, bf16),
            jax.ShapeDtypeStruct(keys.shape, bf16),
            jax.ShapeDtypeStruct(keys.shape, bf16),
        ),
        in_specs=[any_spec] * 4 + [pl.BlockSpec(memory_space=pltpu.VMEM)],
        out_specs=[any_spec] * 4,
        scratch_shapes=[
            pltpu.VMEM((groups, block, wide), bf16),
            pltpu.VMEM((groups, block, wide), bf16),
            pltpu.VMEM((groups, block, wide), bf16),
            pltpu.VMEM((groups, block, wide), bf16),
            pltpu.VMEM((groups, 2, window, HEAD_SIZE), bf16),
            pltpu.VMEM((window, stacked), f32),
            pltpu.VMEM((groups, 2, window, HEAD_SIZE), f32),
            pltpu.VMEM((stacked, HEAD_SIZE), bf16),
            pltpu.VMEM((stacked, HEAD_SIZE), bf16),
            pltpu.VMEM((stacked, HEAD_SIZE), bf16),
            pltpu.VMEM((stacked, HEAD_SIZE), bf16),
            pltpu.VMEM((groups, SLOTS + 1) + pair, bf16),
            pltpu.VMEM((groups, LINE + 1) + pair, bf16),
            pltpu.VMEM((groups, WAYS) + pair, bf16),
            pltpu.VMEM((HEAD_SIZE, window), bf16),
            pltpu.VMEM((HEAD_SIZE, window), bf16),
            pltpu.VMEM((window, stacked), bf16),
            pltpu.VMEM((window, stacked), bf16),
            pltpu.VMEM((stacked, HEAD_SIZE), bf16),
            pltpu.VMEM((2, window, TILE), f32),
            pltpu.VMEM((window, TILE), f32),
            dma((groups, 4)), dma((groups, 4)), dma((groups, 4)),
            dma((groups, 4)), dma((groups, 4)), dma((groups, 4)),
            dma((groups, LINE + 1)), dma((groups, WAYS)), dma((groups, SLOTS + 1)),
            dma((groups, SLOTS + 1)), dma((groups, LINE + 1)), dma((groups, WAYS)),
        ],
        compiler_params=pltpu.CompilerParams(
            collective_id=0, has_side_effects=True, vmem_limit_bytes=56 * 1024 * 1024
        ),
    )(queries, keys, values, output_cotangent, bounds)
    steps = 4
    blocks = [pl.BlockSpec((rows, r.shape[1] // steps), lambda i: (0, i)) for r in results]
    return pl.pallas_call(
        hand_on,
        out_shape=tuple(jax.ShapeDtypeStruct(r.shape, r.dtype) for r in results),
        grid=(steps,),
        in_specs=blocks,
        out_specs=blocks,
    )(*results)


def solution(mesh):
    tokens = P(("seq", "head"), None)
    return jax.shard_map(
        shard,
        mesh=mesh,
        in_specs=(tokens, tokens, tokens, tokens, P()),
        out_specs=(tokens, tokens, tokens, tokens),
        check_vma=False,
    )
```

```python
import functools
import math

import jax
import jax.numpy as jnp
from jax import lax
from jax.experimental import pallas as pl
from jax.experimental.pallas import tpu as pltpu
from jax.sharding import PartitionSpec as P

MESH = pl.DeviceIdType.MESH
HEAD_SIZE = 128
SLOTS = 8
LINE = 4
SCALE = HEAD_SIZE**-0.5
TILE = 256
HIDDEN = -1e30


def dot(left, right, left_dim, right_dim):
    return lax.dot_general(
        left, right, (((left_dim,), (right_dim,)), ((), ())), preferred_element_type=jnp.float32
    )


def hand_on(*refs):
    for i in range(4):
        refs[4 + i][...] = refs[i][...]


def kernel(
    shards, groups, repeat, rows,
    q_ref, k_ref, v_ref, c_ref, bounds_ref,
    out_ref, dq_ref, dk_ref, dv_ref,
    qb, cb, ob, gb, kv, bias, acc, qs, cs, os, gs, stage, from_next, from_line,
    key_t, value_t, e_all, grad_all, cot_n, raw, prob_grad,
    x_send, x_recv, x_local, o_send, o_recv, o_local,
    send_next, send_line, slot_recv, grad_send, next_recv, line_recv,
):
    block = 2 * rows
    window = (SLOTS + 1) * block
    stacked = repeat * block
    wide = repeat * HEAD_SIZE
    s, h = lax.axis_index("seq"), lax.axis_index("head")
    z, k = lax.div(h, 2), lax.rem(h, 2)
    sibling = (s, h + 1 - 2 * k)
    first = s == 0
    has_next, has_prev = s < shards - 1, s > 0
    later, earlier = (s + 1, h), (s - 1, h)

    def exists(j):
        return s * LINE + z >= j

    def goes_next(j):
        return has_next & exists(j) if j <= LINE else None

    def comes_earlier(j):
        return exists(j) if j >= LINE else None

    kinds = ((0, 1), (LINE, -1))
    allowed = (s >= 0, jnp.logical_not(first))

    def there(kind, distance):
        place = z + kinds[kind][1] * distance
        return allowed[kind] & (place >= 0) & (place < LINE)

    def back(kind, distance):
        place = z - kinds[kind][1] * distance
        return allowed[kind] & (place >= 0) & (place < LINE)

    def in_line(kind, distance):
        return (s, h + 2 * kinds[kind][1] * distance)

    def in_line_back(kind, distance):
        return (s, h - 2 * kinds[kind][1] * distance)

    def landing(kind, distance):
        return kinds[kind][0] + kinds[kind][1] * distance

    ways = [(kind, distance) for kind in range(2) for distance in range(1, LINE)]

    def slot(g, j):
        return kv.at[g, :, pl.ds((SLOTS - j) * block, block), :]

    def remote(src, dst, send, recv, device):
        return pltpu.make_async_remote_copy(
            src_ref=src, dst_ref=dst, send_sem=send, recv_sem=recv,
            device_id=device, device_id_type=MESH,
        )

    def when(condition, work):
        if condition is not None:
            pl.when(condition)(work)

    def columns(core, g, width):
        start = (core * groups + g) * width
        return pl.ds(pl.multiple_of(start, HEAD_SIZE), width)

    mine = pl.ds(pl.multiple_of(k * rows, 16), rows)
    theirs = pl.ds(pl.multiple_of((1 - k) * rows, 16), rows)
    mine_tail = pl.ds(pl.multiple_of(SLOTS * block + k * rows, 16), rows)

    def in_place(index, g):
        return (
            lambda: qb.at[g, mine, :], lambda: cb.at[g, mine, :],
            lambda: kv.at[g, 0, mine_tail, :], lambda: kv.at[g, 1, mine_tail, :],
        )[index]()

    def in_copies(index, g):
        source = (q_ref, c_ref, k_ref, v_ref)[index]
        width = wide if index < 2 else HEAD_SIZE
        local = pltpu.make_async_copy(
            source.at[:, columns(k, g, width)], in_place(index, g), x_local.at[g, index]
        )
        over = remote(
            source.at[:, columns(1 - k, g, width)], in_place(index, g),
            x_send.at[g, index], x_recv.at[g, index], sibling,
        )
        return local, over

    def start_in(index, g):
        local, over = in_copies(index, g)
        over.start()
        local.start()

    def wait_in(index, g):
        local, over = in_copies(index, g)
        local.wait()
        over.wait()

    def out_copies(index, g):
        target = (out_ref, dq_ref, dk_ref, dv_ref)[index]
        width = wide if index < 2 else HEAD_SIZE

        def part(which):
            if index < 2:
                return (ob, gb)[index].at[g, which, :]
            return stage.at[g, 0, index - 2, which, :]

        place = target.at[:, columns(k, g, width)]
        local = pltpu.make_async_copy(part(mine), place, o_local.at[g, index])
        over = remote(part(theirs), place, o_send.at[g, index], o_recv.at[g, index], sibling)
        return local, over

    def start_out(index, g):
        local, over = out_copies(index, g)
        over.start()
        local.start()

    def wait_out(index, g):
        local, over = out_copies(index, g)
        local.wait()
        over.wait()

    def next_copy(g, j):
        return remote(
            slot(g, j), slot(g, j + LINE), send_next.at[g, j], slot_recv.at[g, j + LINE], later
        )

    def line_copy(g, kind, distance):
        to = landing(kind, distance)
        return remote(
            slot(g, kinds[kind][0]), slot(g, to), send_line.at[g, ways.index((kind, distance))],
            slot_recv.at[g, to], in_line(kind, distance),
        )

    def forward(g, j):
        for kind, distance in ways:
            if kinds[kind][0] == j:
                when(there(kind, distance), lambda: line_copy(g, kind, distance).start())
        when(goes_next(j), lambda: next_copy(g, j).start())

    def relay(g, j):
        def work():
            remote(
                slot(g, j), slot(g, j), send_next.at[g, 0], slot_recv.at[g, j], sibling
            ).wait_recv()
            forward(g, j)

        when(exists(j), work)

    def each(work, begin=0, count=groups):
        def body(i, _):
            work(begin + i)
            return 0

        lax.fori_loop(0, count, body, 0)

    def out(slots, begin, count=1):
        for j in slots:
            each(lambda g: relay(g, j), begin, count)

    def own(g):
        wait_in(2, g)
        wait_in(3, g)
        forward(g, 0)

    def span(j):
        return pl.ds((SLOTS - j) * block, block)

    def add(g, j, source, sem):
        remote(source, source, grad_send.at[g, 0], sem, sibling).wait_recv()
        acc[g, :, span(j), :] += source[...].astype(jnp.float32)

    def give(g, j, place, sem, device):
        return remote(stage.at[g, j], place, grad_send.at[g, j], sem, device)

    def send_back(g, j, action):
        for index, (kind, distance) in enumerate(ways):
            if landing(kind, distance) == j:
                when(
                    back(kind, distance),
                    lambda: action(
                        give(
                            g, j, from_line.at[g, index], line_recv.at[g, index],
                            in_line_back(kind, distance),
                        )
                    ),
                )
        when(
            comes_earlier(j),
            lambda: action(
                give(g, j, from_next.at[g, j - LINE], next_recv.at[g, j - LINE], earlier)
            ),
        )

    def give_back(g, j, condition):
        def work():
            for index, (kind, distance) in enumerate(ways):
                if kinds[kind][0] == j:
                    when(
                        there(kind, distance),
                        lambda: add(g, j, from_line.at[g, index], line_recv.at[g, index]),
                    )
            when(goes_next(j), lambda: add(g, j, from_next.at[g, j], next_recv.at[g, j]))
            total = acc[g, :, span(j), :]
            if j == 0:
                stage[g, 0, 0] = (total[0] * SCALE).astype(jnp.bfloat16)
                stage[g, 0, 1] = total[1].astype(jnp.bfloat16)
                start_out(2, g)
                start_out(3, g)
            else:
                stage[g, j] = total.astype(jnp.bfloat16)
                send_back(g, j, lambda copy: copy.start())

        when(condition, work)

    def leaves(g):
        for j in range(LINE + 1, SLOTS + 1):
            give_back(g, j, exists(j))

    def home(g, *slots):
        for j in slots:
            give_back(g, j, exists(j))

    def gather_rows(g):
        wait_in(0, g)
        wait_in(1, g)
        for r in range(repeat):
            place = pl.ds(r * block, block)
            cols = pl.ds(r * HEAD_SIZE, HEAD_SIZE)
            qs[place, :] = qb[g, :, cols]
            cs[place, :] = cb[g, :, cols]

    def spread_rows(g):
        for r in range(repeat):
            place = pl.ds(r * block, block)
            cols = pl.ds(r * HEAD_SIZE, HEAD_SIZE)
            ob[g, :, cols] = os[place, :]
            gb[g, :, cols] = gs[place, :]
        start_out(0, g)
        start_out(1, g)

    def attend(g):
        gather_rows(g)
        key, value = kv[g, 0], kv[g, 1]
        key_t[...] = key.T
        value_t[...] = value.T
        tiles = [pl.ds(n * TILE, TILE) for n in range(stacked // TILE)]
        pieces = [pl.ds(i * block, block) for i in range(SLOTS + 1)]
        exponent = SCALE * math.log2(math.e)

        raw[0] = dot(key, qs[tiles[0], :], 1, 1)
        for n, place in enumerate(tiles):
            if n + 1 < len(tiles):
                raw[(n + 1) % 2] = dot(key, qs[tiles[n + 1], :], 1, 1)
            now = raw.at[n % 2]
            top = jnp.full((1, TILE), HIDDEN, jnp.float32)
            for piece in pieces:
                top = jnp.maximum(top, jnp.max(now[piece, :] + bias[piece, place], 0, keepdims=True))
            top = top * exponent
            total = jnp.zeros((1, TILE), jnp.float32)
            for piece in pieces:
                e = jnp.exp2(now[piece, :] * exponent - top + bias[piece, place])
                total = total + jnp.sum(e, 0, keepdims=True)
                e_all[piece, place] = e.astype(jnp.bfloat16)
            inverse = 1.0 / total
            cot_t = (cs[place, :].astype(jnp.float32).T * inverse).astype(jnp.bfloat16)
            cot_n[place, :] = cot_t.astype(jnp.float32).T.astype(jnp.bfloat16)
            prob_grad[...] = dot(value, cot_t, 1, 0)
            out_t = dot(value_t[...], e_all[:, place], 1, 0) * inverse
            out_half = out_t.astype(jnp.bfloat16).astype(jnp.float32)
            delta = jnp.sum(out_half * cot_t.astype(jnp.float32), 0, keepdims=True)
            for piece in pieces:
                e = e_all[piece, place].astype(jnp.float32)
                grad_all[piece, place] = (e * (prob_grad[piece, :] - delta)).astype(jnp.bfloat16)
            query_grad_t = dot(key_t[...], grad_all[:, place], 1, 0) * SCALE
            os[place, :] = out_half.T.astype(jnp.bfloat16)
            gs[place, :] = query_grad_t.T.astype(jnp.bfloat16)
        acc[g, 1] = dot(e_all[...], cot_n[...], 1, 0)
        acc[g, 0] = dot(grad_all[...], qs[...], 1, 0)
        spread_rows(g)

    barrier = pltpu.get_barrier_semaphore()

    def greet(device):
        pl.semaphore_signal(barrier, inc=1, device_id=device, device_id_type=MESH)

    greet(sibling)
    friends = 1
    neighbours = [(has_next, later), (has_prev, earlier)]
    for distance in range(1, LINE):
        neighbours.append((z + distance < LINE, (s, h + 2 * distance)))
        neighbours.append((z >= distance, (s, h - 2 * distance)))
    for near, device in neighbours:
        when(near, lambda: greet(device))
        friends = friends + near.astype(jnp.int32)
    pl.semaphore_wait(barrier, friends)

    def open_keys(g):
        start_in(2, g)
        start_in(3, g)

    def open_rows(g):
        start_in(0, g)
        start_in(1, g)

    def blanks(g):
        for j in range(1, SLOTS + 1):

            def blank(j=j):
                kv[g, :, span(j), :] = jnp.zeros((2, block, HEAD_SIZE), jnp.bfloat16)

            pl.when(jnp.logical_not(exists(j)))(blank)

    each(open_keys)
    each(open_rows)
    own(0)
    each(blanks)
    place = lax.broadcasted_iota(jnp.int32, (window, stacked), 0)
    seen = (place >= bounds_ref[0:1, :]) & (place <= bounds_ref[1:2, :])
    bias[...] = jnp.where(seen, 0.0, HIDDEN)

    def begin(g):
        pl.when(g + 1 < groups)(lambda: own(g + 1))
        relay(g, LINE)

    each(begin)
    out([1, 2, 3], 0, 2)

    def step(i, _):
        @pl.when(i < groups)
        def _():
            out([5, 6, 7, 8], i)
            attend(i)
            leaves(i)

        @pl.when(i + 2 < groups)
        def _():
            out([1, 2, 3], i + 2)

        @pl.when((i >= 1) & (i <= groups))
        def _():
            home(i - 1, 1, 2, 3)

        @pl.when(i >= 2)
        def _():
            home(i - 2, LINE, 0)

        return 0

    lax.fori_loop(0, groups + 2, step, 0)

    def close(g, _):
        for index in range(4):
            wait_out(index, g)
        for j in range(SLOTS + 1):
            when(goes_next(j), lambda: next_copy(g, j).wait_send())
            if j > 0:
                send_back(g, j, lambda copy: copy.wait_send())
        for kind, distance in ways:
            when(there(kind, distance), lambda: line_copy(g, kind, distance).wait_send())
        return 0

    lax.fori_loop(0, groups, close, 0)


def shard(queries, keys, values, output_cotangent, doc_ids):
    shards = lax.axis_size("seq")
    rows = queries.shape[0]
    block = 2 * rows
    window = (SLOTS + 1) * block
    groups = keys.shape[1] // HEAD_SIZE // 2
    repeat = queries.shape[1] // keys.shape[1]
    stacked = repeat * block
    wide = repeat * HEAD_SIZE

    origin = (lax.axis_index("seq") * LINE + lax.axis_index("head") // 2) * block
    base = jnp.maximum(origin - SLOTS * block, 0)
    near = lax.dynamic_slice(doc_ids, (base,), (window,))
    here = lax.dynamic_slice(doc_ids, (origin,), (block,))
    begin = base + jnp.sum((near[None, :] < here[:, None]).astype(jnp.int32), 1)
    begin = begin - (origin - SLOTS * block)
    end = SLOTS * block + jnp.arange(block, dtype=jnp.int32)
    bounds = jnp.stack([jnp.tile(begin, repeat), jnp.tile(end, repeat)])

    bf16, f32 = jnp.bfloat16, jnp.float32
    any_spec = pl.BlockSpec(memory_space=pl.ANY)
    dma = pltpu.SemaphoreType.DMA
    pair = (2, block, HEAD_SIZE)
    results = pl.pallas_call(
        functools.partial(kernel, shards, groups, repeat, rows),
        out_shape=(
            jax.ShapeDtypeStruct(queries.shape, bf16),
            jax.ShapeDtypeStruct(queries.shape, bf16),
            jax.ShapeDtypeStruct(keys.shape, bf16),
            jax.ShapeDtypeStruct(keys.shape, bf16),
        ),
        in_specs=[any_spec] * 4 + [pl.BlockSpec(memory_space=pltpu.VMEM)],
        out_specs=[any_spec] * 4,
        scratch_shapes=[
            pltpu.VMEM((groups, block, wide), bf16),
            pltpu.VMEM((groups, block, wide), bf16),
            pltpu.VMEM((groups, block, wide), bf16),
            pltpu.VMEM((groups, block, wide), bf16),
            pltpu.VMEM((groups, 2, window, HEAD_SIZE), bf16),
            pltpu.VMEM((window, stacked), f32),
            pltpu.VMEM((groups, 2, window, HEAD_SIZE), f32),
            pltpu.VMEM((stacked, HEAD_SIZE), bf16),
            pltpu.VMEM((stacked, HEAD_SIZE), bf16),
            pltpu.VMEM((stacked, HEAD_SIZE), bf16),
            pltpu.VMEM((stacked, HEAD_SIZE), bf16),
            pltpu.VMEM((groups, SLOTS + 1) + pair, bf16),
            pltpu.VMEM((groups, LINE + 1) + pair, bf16),
            pltpu.VMEM((groups, 2 * (LINE - 1)) + pair, bf16),
            pltpu.VMEM((HEAD_SIZE, window), bf16),
            pltpu.VMEM((HEAD_SIZE, window), bf16),
            pltpu.VMEM((window, stacked), bf16),
            pltpu.VMEM((window, stacked), bf16),
            pltpu.VMEM((stacked, HEAD_SIZE), bf16),
            pltpu.VMEM((2, window, TILE), f32),
            pltpu.VMEM((window, TILE), f32),
            dma((groups, 4)), dma((groups, 4)), dma((groups, 4)),
            dma((groups, 4)), dma((groups, 4)), dma((groups, 4)),
            dma((groups, LINE + 1)), dma((groups, 2 * (LINE - 1))), dma((groups, SLOTS + 1)),
            dma((groups, SLOTS + 1)), dma((groups, LINE + 1)), dma((groups, 2 * (LINE - 1))),
        ],
        compiler_params=pltpu.CompilerParams(
            collective_id=0, has_side_effects=True, vmem_limit_bytes=56 * 1024 * 1024
        ),
    )(queries, keys, values, output_cotangent, bounds)
    steps = 4
    blocks = [pl.BlockSpec((rows, r.shape[1] // steps), lambda i: (0, i)) for r in results]
    return pl.pallas_call(
        hand_on,
        out_shape=tuple(jax.ShapeDtypeStruct(r.shape, r.dtype) for r in results),
        grid=(steps,),
        in_specs=blocks,
        out_specs=blocks,
    )(*results)


def solution(mesh):
    tokens = P(("seq", "head"), None)
    return jax.shard_map(
        shard,
        mesh=mesh,
        in_specs=(tokens, tokens, tokens, tokens, P()),
        out_specs=(tokens, tokens, tokens, tokens),
        check_vma=False,
    )
```

```python
import functools
import math

import jax
import jax.numpy as jnp
from jax import lax
from jax.experimental import pallas as pl
from jax.experimental.pallas import tpu as pltpu
from jax.sharding import PartitionSpec as P

MESH = pl.DeviceIdType.MESH
HEAD_SIZE = 128
SLOTS = 8
LINE = 4
SCALE = HEAD_SIZE**-0.5
TILE = 256
HIDDEN = -1e30


def dot(left, right, left_dim, right_dim):
    return lax.dot_general(
        left, right, (((left_dim,), (right_dim,)), ((), ())), preferred_element_type=jnp.float32
    )


def hand_on(*refs):
    for i in range(4):
        refs[4 + i][...] = refs[i][...]


def kernel(
    shards, groups, repeat, rows,
    q_ref, k_ref, v_ref, c_ref, bounds_ref,
    out_ref, dq_ref, dk_ref, dv_ref,
    qb, cb, ob, gb, kv, bias, acc, qs, cs, os, gs, stage, from_next, from_line,
    key_t, value_t, e_all, grad_all, cot_n, raw, prob_grad,
    x_send, x_recv, x_local, o_send, o_recv, o_local,
    send_next, send_line, slot_recv, grad_send, next_recv, line_recv,
):
    block = 2 * rows
    window = (SLOTS + 1) * block
    stacked = repeat * block
    wide = repeat * HEAD_SIZE
    s, h = lax.axis_index("seq"), lax.axis_index("head")
    z, k = lax.div(h, 2), lax.rem(h, 2)
    sibling = (s, h + 1 - 2 * k)
    first, cross, gate = s == 0, s == shards // 2, s == shards // 2 - 1
    has_next, has_prev = s < shards - 1, s > 0
    later, earlier = (s + 1, h), (s - 1, h)

    def exists(j):
        return s * LINE + z >= j

    def goes_next(j):
        if j > LINE:
            return None
        goes = has_next & exists(j)
        return goes if j % LINE == 0 else goes & (jnp.logical_not(gate) | (z < j))

    def comes_earlier(j):
        if j < LINE:
            return None
        return exists(j) if j % LINE == 0 else exists(j) & (jnp.logical_not(cross) | (z < j - LINE))

    kinds = ((0, 1), (LINE, -1), (LINE, 1))
    allowed = (s >= 0, jnp.logical_not(first), cross)

    def there(kind, distance):
        place = z + kinds[kind][1] * distance
        return allowed[kind] & (place >= 0) & (place < LINE)

    def back(kind, distance):
        place = z - kinds[kind][1] * distance
        return allowed[kind] & (place >= 0) & (place < LINE)

    def in_line(kind, distance):
        return (s, h + 2 * kinds[kind][1] * distance)

    def in_line_back(kind, distance):
        return (s, h - 2 * kinds[kind][1] * distance)

    def landing(kind, distance):
        return kinds[kind][0] + kinds[kind][1] * distance

    ways = [(kind, distance) for kind in range(3) for distance in range(1, LINE)]

    def slot(g, j):
        return kv.at[g, :, pl.ds((SLOTS - j) * block, block), :]

    def remote(src, dst, send, recv, device):
        return pltpu.make_async_remote_copy(
            src_ref=src, dst_ref=dst, send_sem=send, recv_sem=recv,
            device_id=device, device_id_type=MESH,
        )

    def when(condition, work):
        if condition is not None:
            pl.when(condition)(work)

    def columns(core, g, width):
        start = (core * groups + g) * width
        return pl.ds(pl.multiple_of(start, HEAD_SIZE), width)

    mine = pl.ds(pl.multiple_of(k * rows, 16), rows)
    theirs = pl.ds(pl.multiple_of((1 - k) * rows, 16), rows)
    mine_tail = pl.ds(pl.multiple_of(SLOTS * block + k * rows, 16), rows)

    def in_place(index, g):
        return (
            lambda: qb.at[g, mine, :], lambda: cb.at[g, mine, :],
            lambda: kv.at[g, 0, mine_tail, :], lambda: kv.at[g, 1, mine_tail, :],
        )[index]()

    def in_copies(index, g):
        source = (q_ref, c_ref, k_ref, v_ref)[index]
        width = wide if index < 2 else HEAD_SIZE
        local = pltpu.make_async_copy(
            source.at[:, columns(k, g, width)], in_place(index, g), x_local.at[g, index]
        )
        over = remote(
            source.at[:, columns(1 - k, g, width)], in_place(index, g),
            x_send.at[g, index], x_recv.at[g, index], sibling,
        )
        return local, over

    def start_in(index, g):
        local, over = in_copies(index, g)
        over.start()
        local.start()

    def wait_in(index, g):
        local, over = in_copies(index, g)
        local.wait()
        over.wait()

    def out_copies(index, g):
        target = (out_ref, dq_ref, dk_ref, dv_ref)[index]
        width = wide if index < 2 else HEAD_SIZE

        def part(which):
            if index < 2:
                return (ob, gb)[index].at[g, which, :]
            return stage.at[g, 0, index - 2, which, :]

        place = target.at[:, columns(k, g, width)]
        local = pltpu.make_async_copy(part(mine), place, o_local.at[g, index])
        over = remote(part(theirs), place, o_send.at[g, index], o_recv.at[g, index], sibling)
        return local, over

    def start_out(index, g):
        local, over = out_copies(index, g)
        over.start()
        local.start()

    def wait_out(index, g):
        local, over = out_copies(index, g)
        local.wait()
        over.wait()

    def next_copy(g, j):
        return remote(
            slot(g, j), slot(g, j + LINE), send_next.at[g, j], slot_recv.at[g, j + LINE], later
        )

    def line_copy(g, kind, distance):
        to = landing(kind, distance)
        return remote(
            slot(g, kinds[kind][0]), slot(g, to), send_line.at[g, ways.index((kind, distance))],
            slot_recv.at[g, to], in_line(kind, distance),
        )

    def forward(g, j):
        for kind, distance in ways:
            if kinds[kind][0] == j:
                when(there(kind, distance), lambda: line_copy(g, kind, distance).start())
        when(goes_next(j), lambda: next_copy(g, j).start())

    def relay(g, j):
        def work():
            remote(
                slot(g, j), slot(g, j), send_next.at[g, 0], slot_recv.at[g, j], sibling
            ).wait_recv()
            forward(g, j)

        when(exists(j), work)

    def each(work, begin=0, count=groups):
        def body(i, _):
            work(begin + i)
            return 0

        lax.fori_loop(0, count, body, 0)

    def out(slots, begin, count=1):
        for j in slots:
            each(lambda g: relay(g, j), begin, count)

    def own(g):
        wait_in(2, g)
        wait_in(3, g)
        forward(g, 0)

    def span(j):
        return pl.ds((SLOTS - j) * block, block)

    def add(g, j, source, sem):
        remote(source, source, grad_send.at[g, 0], sem, sibling).wait_recv()
        acc[g, :, span(j), :] += source[...].astype(jnp.float32)

    def give(g, j, place, sem, device):
        return remote(stage.at[g, j], place, grad_send.at[g, j], sem, device)

    def send_back(g, j, action):
        for index, (kind, distance) in enumerate(ways):
            if landing(kind, distance) == j:
                when(
                    back(kind, distance),
                    lambda: action(
                        give(
                            g, j, from_line.at[g, index], line_recv.at[g, index],
                            in_line_back(kind, distance),
                        )
                    ),
                )
        when(
            comes_earlier(j),
            lambda: action(
                give(g, j, from_next.at[g, j - LINE], next_recv.at[g, j - LINE], earlier)
            ),
        )

    def give_back(g, j, condition):
        def work():
            for index, (kind, distance) in enumerate(ways):
                if kinds[kind][0] == j:
                    when(
                        there(kind, distance),
                        lambda: add(g, j, from_line.at[g, index], line_recv.at[g, index]),
                    )
            when(goes_next(j), lambda: add(g, j, from_next.at[g, j], next_recv.at[g, j]))
            total = acc[g, :, span(j), :]
            if j == 0:
                stage[g, 0, 0] = (total[0] * SCALE).astype(jnp.bfloat16)
                stage[g, 0, 1] = total[1].astype(jnp.bfloat16)
                start_out(2, g)
                start_out(3, g)
            else:
                stage[g, j] = total.astype(jnp.bfloat16)
                send_back(g, j, lambda copy: copy.start())

        when(condition, work)

    def leaves(g):
        for j in range(LINE + 1, SLOTS + 1):
            give_back(g, j, exists(j))

    def home(g, *slots):
        for j in slots:
            give_back(g, j, exists(j))

    def gather_rows(g):
        wait_in(0, g)
        wait_in(1, g)
        for r in range(repeat):
            place = pl.ds(r * block, block)
            cols = pl.ds(r * HEAD_SIZE, HEAD_SIZE)
            qs[place, :] = qb[g, :, cols]
            cs[place, :] = cb[g, :, cols]

    def spread_rows(g):
        for r in range(repeat):
            place = pl.ds(r * block, block)
            cols = pl.ds(r * HEAD_SIZE, HEAD_SIZE)
            ob[g, :, cols] = os[place, :]
            gb[g, :, cols] = gs[place, :]
        start_out(0, g)
        start_out(1, g)

    def attend(g):
        gather_rows(g)
        key, value = kv[g, 0], kv[g, 1]
        key_t[...] = key.T
        value_t[...] = value.T
        tiles = [pl.ds(n * TILE, TILE) for n in range(stacked // TILE)]
        pieces = [pl.ds(i * block, block) for i in range(SLOTS + 1)]
        exponent = SCALE * math.log2(math.e)

        raw[0] = dot(key, qs[tiles[0], :], 1, 1)
        for n, place in enumerate(tiles):
            if n + 1 < len(tiles):
                raw[(n + 1) % 2] = dot(key, qs[tiles[n + 1], :], 1, 1)
            now = raw.at[n % 2]
            top = jnp.full((1, TILE), HIDDEN, jnp.float32)
            for piece in pieces:
                top = jnp.maximum(top, jnp.max(now[piece, :] + bias[piece, place], 0, keepdims=True))
            top = top * exponent
            total = jnp.zeros((1, TILE), jnp.float32)
            for piece in pieces:
                e = jnp.exp2(now[piece, :] * exponent - top + bias[piece, place])
                total = total + jnp.sum(e, 0, keepdims=True)
                e_all[piece, place] = e.astype(jnp.bfloat16)
            inverse = 1.0 / total
            cot_t = (cs[place, :].astype(jnp.float32).T * inverse).astype(jnp.bfloat16)
            cot_n[place, :] = cot_t.astype(jnp.float32).T.astype(jnp.bfloat16)
            prob_grad[...] = dot(value, cot_t, 1, 0)
            out_t = dot(value_t[...], e_all[:, place], 1, 0) * inverse
            out_half = out_t.astype(jnp.bfloat16).astype(jnp.float32)
            delta = jnp.sum(out_half * cot_t.astype(jnp.float32), 0, keepdims=True)
            for piece in pieces:
                e = e_all[piece, place].astype(jnp.float32)
                grad_all[piece, place] = (e * (prob_grad[piece, :] - delta)).astype(jnp.bfloat16)
            query_grad_t = dot(key_t[...], grad_all[:, place], 1, 0) * SCALE
            os[place, :] = out_half.T.astype(jnp.bfloat16)
            gs[place, :] = query_grad_t.T.astype(jnp.bfloat16)
        acc[g, 1] = dot(e_all[...], cot_n[...], 1, 0)
        acc[g, 0] = dot(grad_all[...], qs[...], 1, 0)
        spread_rows(g)

    barrier = pltpu.get_barrier_semaphore()

    def greet(device):
        pl.semaphore_signal(barrier, inc=1, device_id=device, device_id_type=MESH)

    greet(sibling)
    friends = 1
    neighbours = [(has_next, later), (has_prev, earlier)]
    for distance in range(1, LINE):
        neighbours.append((z + distance < LINE, (s, h + 2 * distance)))
        neighbours.append((z >= distance, (s, h - 2 * distance)))
    for near, device in neighbours:
        when(near, lambda: greet(device))
        friends = friends + near.astype(jnp.int32)
    pl.semaphore_wait(barrier, friends)

    def open_keys(g):
        start_in(2, g)
        start_in(3, g)

    def open_rows(g):
        start_in(0, g)
        start_in(1, g)

    def blanks(g):
        for j in range(1, SLOTS + 1):

            def blank(j=j):
                kv[g, :, span(j), :] = jnp.zeros((2, block, HEAD_SIZE), jnp.bfloat16)

            pl.when(jnp.logical_not(exists(j)))(blank)

    each(open_keys)
    each(open_rows)
    own(0)
    each(blanks)
    place = lax.broadcasted_iota(jnp.int32, (window, stacked), 0)
    seen = (place >= bounds_ref[0:1, :]) & (place <= bounds_ref[1:2, :])
    bias[...] = jnp.where(seen, 0.0, HIDDEN)

    def begin(g):
        pl.when(g + 1 < groups)(lambda: own(g + 1))
        relay(g, LINE)

    each(begin)
    out([1, 2, 3], 0, 2)

    def step(i, _):
        @pl.when(i < groups)
        def _():
            out([5, 6, 7, 8], i)
            attend(i)
            leaves(i)

        @pl.when(i + 2 < groups)
        def _():
            out([1, 2, 3], i + 2)

        @pl.when(i >= 2)
        def _():
            home(i - 2, 1, 2, 3)

        @pl.when(i >= groups)
        def _():
            home(i - groups, LINE, 0)

        return 0

    lax.fori_loop(0, groups + 2, step, 0)
    each(lambda g: home(g, LINE, 0), 2, groups - 2)

    def close(g, _):
        for index in range(4):
            wait_out(index, g)
        for j in range(SLOTS + 1):
            when(goes_next(j), lambda: next_copy(g, j).wait_send())
            if j > 0:
                send_back(g, j, lambda copy: copy.wait_send())
        for kind, distance in ways:
            when(there(kind, distance), lambda: line_copy(g, kind, distance).wait_send())
        return 0

    lax.fori_loop(0, groups, close, 0)


def shard(queries, keys, values, output_cotangent, doc_ids):
    shards = lax.axis_size("seq")
    rows = queries.shape[0]
    block = 2 * rows
    window = (SLOTS + 1) * block
    groups = keys.shape[1] // HEAD_SIZE // 2
    repeat = queries.shape[1] // keys.shape[1]
    stacked = repeat * block
    wide = repeat * HEAD_SIZE

    origin = (lax.axis_index("seq") * LINE + lax.axis_index("head") // 2) * block
    base = jnp.maximum(origin - SLOTS * block, 0)
    near = lax.dynamic_slice(doc_ids, (base,), (window,))
    here = lax.dynamic_slice(doc_ids, (origin,), (block,))
    begin = base + jnp.sum((near[None, :] < here[:, None]).astype(jnp.int32), 1)
    begin = begin - (origin - SLOTS * block)
    end = SLOTS * block + jnp.arange(block, dtype=jnp.int32)
    bounds = jnp.stack([jnp.tile(begin, repeat), jnp.tile(end, repeat)])

    bf16, f32 = jnp.bfloat16, jnp.float32
    any_spec = pl.BlockSpec(memory_space=pl.ANY)
    dma = pltpu.SemaphoreType.DMA
    pair = (2, block, HEAD_SIZE)
    results = pl.pallas_call(
        functools.partial(kernel, shards, groups, repeat, rows),
        out_shape=(
            jax.ShapeDtypeStruct(queries.shape, bf16),
            jax.ShapeDtypeStruct(queries.shape, bf16),
            jax.ShapeDtypeStruct(keys.shape, bf16),
            jax.ShapeDtypeStruct(keys.shape, bf16),
        ),
        in_specs=[any_spec] * 4 + [pl.BlockSpec(memory_space=pltpu.VMEM)],
        out_specs=[any_spec] * 4,
        scratch_shapes=[
            pltpu.VMEM((groups, block, wide), bf16),
            pltpu.VMEM((groups, block, wide), bf16),
            pltpu.VMEM((groups, block, wide), bf16),
            pltpu.VMEM((groups, block, wide), bf16),
            pltpu.VMEM((groups, 2, window, HEAD_SIZE), bf16),
            pltpu.VMEM((window, stacked), f32),
            pltpu.VMEM((groups, 2, window, HEAD_SIZE), f32),
            pltpu.VMEM((stacked, HEAD_SIZE), bf16),
            pltpu.VMEM((stacked, HEAD_SIZE), bf16),
            pltpu.VMEM((stacked, HEAD_SIZE), bf16),
            pltpu.VMEM((stacked, HEAD_SIZE), bf16),
            pltpu.VMEM((groups, SLOTS + 1) + pair, bf16),
            pltpu.VMEM((groups, LINE + 1) + pair, bf16),
            pltpu.VMEM((groups, 3 * (LINE - 1)) + pair, bf16),
            pltpu.VMEM((HEAD_SIZE, window), bf16),
            pltpu.VMEM((HEAD_SIZE, window), bf16),
            pltpu.VMEM((window, stacked), bf16),
            pltpu.VMEM((window, stacked), bf16),
            pltpu.VMEM((stacked, HEAD_SIZE), bf16),
            pltpu.VMEM((2, window, TILE), f32),
            pltpu.VMEM((window, TILE), f32),
            dma((groups, 4)), dma((groups, 4)), dma((groups, 4)),
            dma((groups, 4)), dma((groups, 4)), dma((groups, 4)),
            dma((groups, LINE + 1)), dma((groups, 3 * (LINE - 1))), dma((groups, SLOTS + 1)),
            dma((groups, SLOTS + 1)), dma((groups, LINE + 1)), dma((groups, 3 * (LINE - 1))),
        ],
        compiler_params=pltpu.CompilerParams(
            collective_id=0, has_side_effects=True, vmem_limit_bytes=56 * 1024 * 1024
        ),
    )(queries, keys, values, output_cotangent, bounds)
    steps = 4
    blocks = [pl.BlockSpec((rows, r.shape[1] // steps), lambda i: (0, i)) for r in results]
    return pl.pallas_call(
        hand_on,
        out_shape=tuple(jax.ShapeDtypeStruct(r.shape, r.dtype) for r in results),
        grid=(steps,),
        in_specs=blocks,
        out_specs=blocks,
    )(*results)


def solution(mesh):
    tokens = P(("seq", "head"), None)
    return jax.shard_map(
        shard,
        mesh=mesh,
        in_specs=(tokens, tokens, tokens, tokens, P()),
        out_specs=(tokens, tokens, tokens, tokens),
        check_vma=False,
    )
```

```python
import functools
import math

import jax
import jax.numpy as jnp
from jax import lax
from jax.experimental import pallas as pl
from jax.experimental.pallas import tpu as pltpu
from jax.sharding import PartitionSpec as P

MESH = pl.DeviceIdType.MESH
HEAD_SIZE = 128
SLOTS = 8
LINE = 4
SCALE = HEAD_SIZE**-0.5
TILE = 256
HIDDEN = -1e30


def dot(left, right, left_dim, right_dim):
    return lax.dot_general(
        left, right, (((left_dim,), (right_dim,)), ((), ())), preferred_element_type=jnp.float32
    )


def hand_on(*refs):
    for i in range(4):
        refs[4 + i][...] = refs[i][...]


def kernel(
    shards, groups, repeat, rows,
    q_ref, k_ref, v_ref, c_ref, bounds_ref,
    out_ref, dq_ref, dk_ref, dv_ref,
    qb, cb, ob, gb, kv, bias, acc, qs, cs, os, gs, stage, from_next, from_line,
    key_t, value_t, e_all, grad_all, cot_n, raw, prob_grad,
    x_send, x_recv, x_local, o_send, o_recv, o_local,
    send_next, send_line, slot_recv, grad_send, next_recv, line_recv,
):
    block = 2 * rows
    window = (SLOTS + 1) * block
    stacked = repeat * block
    wide = repeat * HEAD_SIZE
    s, h = lax.axis_index("seq"), lax.axis_index("head")
    z, k = lax.div(h, 2), lax.rem(h, 2)
    sibling = (s, h + 1 - 2 * k)
    first, cross, gate = s == 0, s == shards // 2, s == shards // 2 - 1
    has_next, has_prev = s < shards - 1, s > 0
    later, earlier = (s + 1, h), (s - 1, h)

    def exists(j):
        return s * LINE + z >= j

    def goes_next(j):
        if j > LINE:
            return None
        goes = has_next & exists(j)
        return goes if j % LINE == 0 else goes & (jnp.logical_not(gate) | (z == 0))

    def comes_earlier(j):
        if j < LINE:
            return None
        return exists(j) if j % LINE == 0 else exists(j) & (jnp.logical_not(cross) | (z == 0))

    kinds = ((0, 1), (LINE, -1), (LINE, 1), (SLOTS, -1))
    allowed = (s >= 0, jnp.logical_not(first), cross, cross)
    lowest = (0, 0, 0, 1)

    def there(kind, distance):
        place = z + kinds[kind][1] * distance
        return allowed[kind] & (place >= lowest[kind]) & (place < LINE)

    def back(kind, distance):
        place = z - kinds[kind][1] * distance
        return allowed[kind] & (place >= 0) & (place < LINE) & (z >= lowest[kind])

    def in_line(kind, distance):
        return (s, h + 2 * kinds[kind][1] * distance)

    def in_line_back(kind, distance):
        return (s, h - 2 * kinds[kind][1] * distance)

    def landing(kind, distance):
        return kinds[kind][0] + kinds[kind][1] * distance

    ways = [(kind, distance) for kind in range(4) for distance in range(1, LINE)]

    def slot(g, j):
        return kv.at[g, :, pl.ds((SLOTS - j) * block, block), :]

    def remote(src, dst, send, recv, device):
        return pltpu.make_async_remote_copy(
            src_ref=src, dst_ref=dst, send_sem=send, recv_sem=recv,
            device_id=device, device_id_type=MESH,
        )

    def when(condition, work):
        if condition is not None:
            pl.when(condition)(work)

    def columns(core, g, width):
        start = (core * groups + g) * width
        return pl.ds(pl.multiple_of(start, HEAD_SIZE), width)

    mine = pl.ds(pl.multiple_of(k * rows, 16), rows)
    theirs = pl.ds(pl.multiple_of((1 - k) * rows, 16), rows)
    mine_tail = pl.ds(pl.multiple_of(SLOTS * block + k * rows, 16), rows)

    def in_place(index, g):
        return (
            lambda: qb.at[g, mine, :], lambda: cb.at[g, mine, :],
            lambda: kv.at[g, 0, mine_tail, :], lambda: kv.at[g, 1, mine_tail, :],
        )[index]()

    def in_copies(index, g):
        source = (q_ref, c_ref, k_ref, v_ref)[index]
        width = wide if index < 2 else HEAD_SIZE
        local = pltpu.make_async_copy(
            source.at[:, columns(k, g, width)], in_place(index, g), x_local.at[g, index]
        )
        over = remote(
            source.at[:, columns(1 - k, g, width)], in_place(index, g),
            x_send.at[g, index], x_recv.at[g, index], sibling,
        )
        return local, over

    def start_in(index, g):
        local, over = in_copies(index, g)
        over.start()
        local.start()

    def wait_in(index, g):
        local, over = in_copies(index, g)
        local.wait()
        over.wait()

    def out_copies(index, g):
        target = (out_ref, dq_ref, dk_ref, dv_ref)[index]
        width = wide if index < 2 else HEAD_SIZE

        def part(which):
            if index < 2:
                return (ob, gb)[index].at[g, which, :]
            return stage.at[g, 0, index - 2, which, :]

        place = target.at[:, columns(k, g, width)]
        local = pltpu.make_async_copy(part(mine), place, o_local.at[g, index])
        over = remote(part(theirs), place, o_send.at[g, index], o_recv.at[g, index], sibling)
        return local, over

    def start_out(index, g):
        local, over = out_copies(index, g)
        over.start()
        local.start()

    def wait_out(index, g):
        local, over = out_copies(index, g)
        local.wait()
        over.wait()

    def next_copy(g, j):
        return remote(
            slot(g, j), slot(g, j + LINE), send_next.at[g, j], slot_recv.at[g, j + LINE], later
        )

    def line_copy(g, kind, distance):
        to = landing(kind, distance)
        return remote(
            slot(g, kinds[kind][0]), slot(g, to), send_line.at[g, ways.index((kind, distance))],
            slot_recv.at[g, to], in_line(kind, distance),
        )

    def forward(g, j):
        for kind, distance in ways:
            if kinds[kind][0] == j:
                when(there(kind, distance), lambda: line_copy(g, kind, distance).start())
        when(goes_next(j), lambda: next_copy(g, j).start())

    def relay(g, j):
        def work():
            remote(
                slot(g, j), slot(g, j), send_next.at[g, 0], slot_recv.at[g, j], sibling
            ).wait_recv()
            forward(g, j)

        when(exists(j), work)

    def each(work, begin=0, count=groups):
        def body(i, _):
            work(begin + i)
            return 0

        lax.fori_loop(0, count, body, 0)

    def out(slots, begin, count=1):
        for j in slots:
            each(lambda g: relay(g, j), begin, count)

    def own(g):
        wait_in(2, g)
        wait_in(3, g)
        forward(g, 0)

    def span(j):
        return pl.ds((SLOTS - j) * block, block)

    def add(g, j, source, sem):
        remote(source, source, grad_send.at[g, 0], sem, sibling).wait_recv()
        acc[g, :, span(j), :] += source[...].astype(jnp.float32)

    def give(g, j, place, sem, device):
        return remote(stage.at[g, j], place, grad_send.at[g, j], sem, device)

    def send_back(g, j, action):
        for index, (kind, distance) in enumerate(ways):
            if landing(kind, distance) == j:
                when(
                    back(kind, distance),
                    lambda: action(
                        give(
                            g, j, from_line.at[g, index], line_recv.at[g, index],
                            in_line_back(kind, distance),
                        )
                    ),
                )
        when(
            comes_earlier(j),
            lambda: action(
                give(g, j, from_next.at[g, j - LINE], next_recv.at[g, j - LINE], earlier)
            ),
        )

    def give_back(g, j, condition):
        def work():
            for index, (kind, distance) in enumerate(ways):
                if kinds[kind][0] == j:
                    when(
                        there(kind, distance),
                        lambda: add(g, j, from_line.at[g, index], line_recv.at[g, index]),
                    )
            when(goes_next(j), lambda: add(g, j, from_next.at[g, j], next_recv.at[g, j]))
            total = acc[g, :, span(j), :]
            if j == 0:
                stage[g, 0, 0] = (total[0] * SCALE).astype(jnp.bfloat16)
                stage[g, 0, 1] = total[1].astype(jnp.bfloat16)
                start_out(2, g)
                start_out(3, g)
            else:
                stage[g, j] = total.astype(jnp.bfloat16)
                send_back(g, j, lambda copy: copy.start())

        when(condition, work)

    chained = cross & (z >= 2)

    def leaves(g):
        for j in range(LINE + 1, SLOTS):
            give_back(g, j, exists(j))
        give_back(g, SLOTS, exists(SLOTS) & jnp.logical_not(chained))

    def home(g, *slots):
        for j in slots:
            give_back(g, j, chained if j == SLOTS else exists(j))

    def gather_rows(g):
        wait_in(0, g)
        wait_in(1, g)
        for r in range(repeat):
            place = pl.ds(r * block, block)
            cols = pl.ds(r * HEAD_SIZE, HEAD_SIZE)
            qs[place, :] = qb[g, :, cols]
            cs[place, :] = cb[g, :, cols]

    def spread_rows(g):
        for r in range(repeat):
            place = pl.ds(r * block, block)
            cols = pl.ds(r * HEAD_SIZE, HEAD_SIZE)
            ob[g, :, cols] = os[place, :]
            gb[g, :, cols] = gs[place, :]
        start_out(0, g)
        start_out(1, g)

    def attend(g):
        gather_rows(g)
        key, value = kv[g, 0], kv[g, 1]
        key_t[...] = key.T
        value_t[...] = value.T
        tiles = [pl.ds(n * TILE, TILE) for n in range(stacked // TILE)]
        pieces = [pl.ds(i * block, block) for i in range(SLOTS + 1)]
        exponent = SCALE * math.log2(math.e)

        raw[0] = dot(key, qs[tiles[0], :], 1, 1)
        for n, place in enumerate(tiles):
            if n + 1 < len(tiles):
                raw[(n + 1) % 2] = dot(key, qs[tiles[n + 1], :], 1, 1)
            now = raw.at[n % 2]
            top = jnp.full((1, TILE), HIDDEN, jnp.float32)
            for piece in pieces:
                top = jnp.maximum(top, jnp.max(now[piece, :] + bias[piece, place], 0, keepdims=True))
            top = top * exponent
            total = jnp.zeros((1, TILE), jnp.float32)
            for piece in pieces:
                e = jnp.exp2(now[piece, :] * exponent - top + bias[piece, place])
                total = total + jnp.sum(e, 0, keepdims=True)
                e_all[piece, place] = e.astype(jnp.bfloat16)
            inverse = 1.0 / total
            cot_t = (cs[place, :].astype(jnp.float32).T * inverse).astype(jnp.bfloat16)
            cot_n[place, :] = cot_t.astype(jnp.float32).T.astype(jnp.bfloat16)
            prob_grad[...] = dot(value, cot_t, 1, 0)
            out_t = dot(value_t[...], e_all[:, place], 1, 0) * inverse
            out_half = out_t.astype(jnp.bfloat16).astype(jnp.float32)
            delta = jnp.sum(out_half * cot_t.astype(jnp.float32), 0, keepdims=True)
            for piece in pieces:
                e = e_all[piece, place].astype(jnp.float32)
                grad_all[piece, place] = (e * (prob_grad[piece, :] - delta)).astype(jnp.bfloat16)
            query_grad_t = dot(key_t[...], grad_all[:, place], 1, 0) * SCALE
            os[place, :] = out_half.T.astype(jnp.bfloat16)
            gs[place, :] = query_grad_t.T.astype(jnp.bfloat16)
        acc[g, 1] = dot(e_all[...], cot_n[...], 1, 0)
        acc[g, 0] = dot(grad_all[...], qs[...], 1, 0)
        spread_rows(g)

    barrier = pltpu.get_barrier_semaphore()

    def greet(device):
        pl.semaphore_signal(barrier, inc=1, device_id=device, device_id_type=MESH)

    greet(sibling)
    friends = 1
    neighbours = [(has_next, later), (has_prev, earlier)]
    for distance in range(1, LINE):
        neighbours.append((z + distance < LINE, (s, h + 2 * distance)))
        neighbours.append((z >= distance, (s, h - 2 * distance)))
    for near, device in neighbours:
        when(near, lambda: greet(device))
        friends = friends + near.astype(jnp.int32)
    pl.semaphore_wait(barrier, friends)

    def open_keys(g):
        start_in(2, g)
        start_in(3, g)

    def open_rows(g):
        start_in(0, g)
        start_in(1, g)

    def blanks(g):
        for j in range(1, SLOTS + 1):

            def blank(j=j):
                kv[g, :, span(j), :] = jnp.zeros((2, block, HEAD_SIZE), jnp.bfloat16)

            pl.when(jnp.logical_not(exists(j)))(blank)

    each(open_keys)
    each(open_rows)
    own(0)
    each(blanks)
    place = lax.broadcasted_iota(jnp.int32, (window, stacked), 0)
    seen = (place >= bounds_ref[0:1, :]) & (place <= bounds_ref[1:2, :])
    bias[...] = jnp.where(seen, 0.0, HIDDEN)

    def begin(g):
        pl.when(g + 1 < groups)(lambda: own(g + 1))
        relay(g, LINE)

    each(begin)
    out([1, 2, 3], 0, 2)
    out([SLOTS], 0)

    def step(i, _):
        @pl.when(i < groups)
        def _():
            out([5, 6, 7], i)
            pl.when(i + 1 < groups)(lambda: out([SLOTS], i + 1))
            attend(i)
            leaves(i)

        @pl.when(i + 2 < groups)
        def _():
            out([1, 2, 3], i + 2)

        @pl.when(i >= 2)
        def _():
            home(i - 2, SLOTS, 1, 2, 3)

        @pl.when(i >= groups)
        def _():
            home(i - groups, LINE, 0)

        return 0

    lax.fori_loop(0, groups + 2, step, 0)
    each(lambda g: home(g, LINE, 0), 2, groups - 2)

    def close(g, _):
        for index in range(4):
            wait_out(index, g)
        for j in range(SLOTS + 1):
            when(goes_next(j), lambda: next_copy(g, j).wait_send())
            if j > 0:
                send_back(g, j, lambda copy: copy.wait_send())
        for kind, distance in ways:
            when(there(kind, distance), lambda: line_copy(g, kind, distance).wait_send())
        return 0

    lax.fori_loop(0, groups, close, 0)


def shard(queries, keys, values, output_cotangent, doc_ids):
    shards = lax.axis_size("seq")
    rows = queries.shape[0]
    block = 2 * rows
    window = (SLOTS + 1) * block
    groups = keys.shape[1] // HEAD_SIZE // 2
    repeat = queries.shape[1] // keys.shape[1]
    stacked = repeat * block
    wide = repeat * HEAD_SIZE

    origin = (lax.axis_index("seq") * LINE + lax.axis_index("head") // 2) * block
    base = jnp.maximum(origin - SLOTS * block, 0)
    near = lax.dynamic_slice(doc_ids, (base,), (window,))
    here = lax.dynamic_slice(doc_ids, (origin,), (block,))
    begin = base + jnp.sum((near[None, :] < here[:, None]).astype(jnp.int32), 1)
    begin = begin - (origin - SLOTS * block)
    end = SLOTS * block + jnp.arange(block, dtype=jnp.int32)
    bounds = jnp.stack([jnp.tile(begin, repeat), jnp.tile(end, repeat)])

    bf16, f32 = jnp.bfloat16, jnp.float32
    any_spec = pl.BlockSpec(memory_space=pl.ANY)
    dma = pltpu.SemaphoreType.DMA
    pair = (2, block, HEAD_SIZE)
    results = pl.pallas_call(
        functools.partial(kernel, shards, groups, repeat, rows),
        out_shape=(
            jax.ShapeDtypeStruct(queries.shape, bf16),
            jax.ShapeDtypeStruct(queries.shape, bf16),
            jax.ShapeDtypeStruct(keys.shape, bf16),
            jax.ShapeDtypeStruct(keys.shape, bf16),
        ),
        in_specs=[any_spec] * 4 + [pl.BlockSpec(memory_space=pltpu.VMEM)],
        out_specs=[any_spec] * 4,
        scratch_shapes=[
            pltpu.VMEM((groups, block, wide), bf16),
            pltpu.VMEM((groups, block, wide), bf16),
            pltpu.VMEM((groups, block, wide), bf16),
            pltpu.VMEM((groups, block, wide), bf16),
            pltpu.VMEM((groups, 2, window, HEAD_SIZE), bf16),
            pltpu.VMEM((window, stacked), f32),
            pltpu.VMEM((groups, 2, window, HEAD_SIZE), f32),
            pltpu.VMEM((stacked, HEAD_SIZE), bf16),
            pltpu.VMEM((stacked, HEAD_SIZE), bf16),
            pltpu.VMEM((stacked, HEAD_SIZE), bf16),
            pltpu.VMEM((stacked, HEAD_SIZE), bf16),
            pltpu.VMEM((groups, SLOTS + 1) + pair, bf16),
            pltpu.VMEM((groups, LINE + 1) + pair, bf16),
            pltpu.VMEM((groups, 4 * (LINE - 1)) + pair, bf16),
            pltpu.VMEM((HEAD_SIZE, window), bf16),
            pltpu.VMEM((HEAD_SIZE, window), bf16),
            pltpu.VMEM((window, stacked), bf16),
            pltpu.VMEM((window, stacked), bf16),
            pltpu.VMEM((stacked, HEAD_SIZE), bf16),
            pltpu.VMEM((2, window, TILE), f32),
            pltpu.VMEM((window, TILE), f32),
            dma((groups, 4)), dma((groups, 4)), dma((groups, 4)),
            dma((groups, 4)), dma((groups, 4)), dma((groups, 4)),
            dma((groups, LINE + 1)), dma((groups, 4 * (LINE - 1))), dma((groups, SLOTS + 1)),
            dma((groups, SLOTS + 1)), dma((groups, LINE + 1)), dma((groups, 4 * (LINE - 1))),
        ],
        compiler_params=pltpu.CompilerParams(
            collective_id=0, has_side_effects=True, vmem_limit_bytes=56 * 1024 * 1024
        ),
    )(queries, keys, values, output_cotangent, bounds)
    steps = 4
    blocks = [pl.BlockSpec((rows, r.shape[1] // steps), lambda i: (0, i)) for r in results]
    return pl.pallas_call(
        hand_on,
        out_shape=tuple(jax.ShapeDtypeStruct(r.shape, r.dtype) for r in results),
        grid=(steps,),
        in_specs=blocks,
        out_specs=blocks,
    )(*results)


def solution(mesh):
    tokens = P(("seq", "head"), None)
    return jax.shard_map(
        shard,
        mesh=mesh,
        in_specs=(tokens, tokens, tokens, tokens, P()),
        out_specs=(tokens, tokens, tokens, tokens),
        check_vma=False,
    )
```
